512 devices in a mesh: col: 16 (over z, x_lo), sample: 32 (over x_hi, y, core).
Axes of the slice: x: 4 (x_hi: 2, x_lo: 2; x = x_hi * 2 + x_lo), y: 8, z: 8, core: 2. Of those that a mesh axis runs over, the one named last changes fastest.
Arguments:
- interaction: bfloat16 [2304, 8192], P('col', 'sample'), may hold values from -6 to 6
- out_grad: bfloat16 [8192, 4096], P('sample', 'col'), may hold values from -0.06591797 to 0.06591797
- top_weight: bfloat16 [2304, 4096], P(None, 'col'), may hold values from -0.125 to 0.125
- pooled: bfloat16 [48, 128, 8192], P(None, 'col', 'sample'), may hold values from -6 to 6
- bags: int32 [48, 4, 8192], P(None, None, 'sample'), may hold values from 0 to 511
- row_place: int32 [48, 512], replicated, may hold values from 0 to 511, each once within a row
Outputs:
- weight_grad: float32 [2304, 4096], P('sample', 'col')
- table_grad: float32 [128, 48, 512], P('col', None, 'sample')
The draws below stay inside these ranges and needn't reach their ends.
Inputs may be any that keep to these rules, and one draw needn't show every extreme that they name: Each row of row_place holds every position 0 to 511 once.
All inputs are finite; a program needn't handle non-finite values.
Results may differ from the reference program's by a relative error of at most 0.0029.
Values may be sent and summed in bfloat16 or wider, within the bound.
A program may use at most 64 MiB of HBM per device.

```python
import math
import jax
import jax.numpy as jnp
import numpy as np
from jax import lax

F = 48
E = 128
H = 4096
L = 4
SB = 256
RPD = 16
FF = 2304
B = 8192
RT = 512
N_COL = 16
N_SAMPLE = 32


def set_ends(entries, key, low, high):
    longest = entries.shape.index(max(entries.shape))
    spots = []
    for shift in (0, 1):
        where = [jax.random.randint(jax.random.fold_in(key, axis), (), 0, length) for axis, length in enumerate(entries.shape)]
        where[longest] = (where[longest] + shift) % entries.shape[longest]
        spots.append(tuple(where))
    return entries.at[spots[0]].set(low).at[spots[1]].set(high)


def level_of(stream_key, shape, cuts, smallest, largest):
    factor_of, own = 1.0, jax.random.fold_in(stream_key, 6)
    for position, blocks in cuts:
        draws = jnp.exp(jax.random.uniform(jax.random.fold_in(own, position), (blocks,), jnp.float32, smallest / len(cuts), largest / len(cuts)))
        factor_of = factor_of * jnp.repeat(draws, shape[position] // blocks).reshape([-1 if axis == position else 1 for axis in range(len(shape))])
    return factor_of


def rank_table(count, skew):
    portions = [(1 << 20) // math.isqrt(standing ** skew) + 1 for standing in range(1, count + 1)]
    scale = 1 + sum(portions) // (1 << 30)
    return np.cumsum(np.array([max(1, weight // scale) for weight in portions]))


def skewed_ids(rng, extent, number_of, slope):
    grid = rank_table(number_of, slope)
    lot = jax.random.randint(jax.random.fold_in(rng, 1), extent, 0, int(grid[number_of - 1]))
    grade = jnp.searchsorted(jnp.asarray(grid, jnp.int32), lot, side="right")
    return jax.random.permutation(jax.random.fold_in(rng, 2), number_of)[grade].astype(jnp.int32)


def centred(stream_key, shape, scale, most, split=(), kind=jnp.bfloat16):
    entries = jax.random.normal(stream_key, shape, jnp.float32) * scale
    if len(split) > 0:
        entries = level_of(stream_key, shape, split, -0.22, 0.18) * entries
    return jnp.clip(entries, min=-most, max=most).astype(kind)


def setup_inputs(seed: int = 0) -> dict:
    splits = jax.random.split(jax.random.key(seed), 7)
    interaction = centred(splits[0], (FF, B), 1.0, 6.0, ((0, 16), (1, 32)))
    out_grad = centred(splits[1], (B, H), ((SB * N_SAMPLE) ** -0.5), 0.06591797, ((0, 32), (1, 16)))
    top_weight = centred(splits[2], (FF, H), (F * F) ** -0.5, 0.125, ((1, 16),))
    pooled = centred(splits[3], (F, E, B), 1.0, 6.0, ((1, 16), (2, 32)))
    bags = set_ends(skewed_ids(splits[4], (F, L, B), RPD * N_SAMPLE, 1), jax.random.fold_in(splits[4], 3), 0, (RPD * N_SAMPLE) - 1).astype(jnp.int32)
    row_place = jax.vmap(lambda own: jax.random.permutation(own, RPD * N_SAMPLE))(jax.random.split(splits[5], F)).reshape((F, RT)).astype(jnp.int32)
    return dict(interaction=interaction, out_grad=out_grad, top_weight=top_weight, pooled=pooled, bags=bags, row_place=row_place)


def reference(interaction, out_grad, top_weight, pooled, bags, row_place):
    group_width = H // N_COL
    samples = SB * N_SAMPLE
    row_count = RPD * N_SAMPLE
    gram_wide = jnp.zeros((F, F, samples), jnp.float32)
    for column in range(N_COL):
        weight_part = top_weight[:, column * group_width:(column + 1) * group_width]
        grad_part = out_grad[:, column * group_width:(column + 1) * group_width]
        partial_value = lax.dot_general(weight_part, grad_part, (((1,), (1,)), ((), ())), preferred_element_type=jnp.float32)
        grad_cube = partial_value.reshape(F, F, samples)
        gram_wide = gram_wide + (grad_cube + jnp.transpose(grad_cube, (1, 0, 2)))
    gram_grad = gram_wide.astype(jnp.bfloat16)
    gram_grad = lax.optimization_barrier(gram_grad)
    gram_wide = gram_grad.astype(jnp.float32)
    pooled_wide = pooled.astype(jnp.float32)
    places = jnp.take_along_axis(row_place, bags.reshape(F, L * samples), axis=1).reshape(F, L, samples)

    def per_feature(inputs):
        gram_row, place_row = inputs
        row_grad = jnp.einsum("jb,jeb->eb", gram_row, pooled_wide)
        table_part = jnp.zeros((E, row_count), jnp.float32)
        for bag_slot in range(L):
            table_part = table_part.at[:, place_row[bag_slot]].add(row_grad)
        return table_part

    tables = lax.map(per_feature, (gram_wide, places))
    table_grad = jnp.transpose(tables, (1, 0, 2))
    weight_grad = jnp.dot(interaction, out_grad, preferred_element_type=jnp.float32)
    return weight_grad, table_grad
```

```python
import jax
import jax.numpy as jnp
from jax import lax
from jax.experimental import pallas as pl
from jax.experimental.pallas import tpu as pltpu
from jax.sharding import PartitionSpec as P

MESH = pl.DeviceIdType.MESH
F32, BF16, I32 = jnp.float32, jnp.bfloat16, jnp.int32

F, E8, SB, HB, L, RT = 48, 8, 256, 256, 4, 512
NZ, NX, NY = 8, 2, 8
OFF = F // 2 + 1
CH = 80
WR = 72
IR = 144
GF = 16
NG = F // GF
EXT = F + F // 2
NT = (((1,), (1,)), ((), ()))


def swap_groups(v, rows, lanes):
    for k in (2, 1, 0):
        step = 1 << k
        up = (rows & step) == 0
        left = (lanes & (16 * step)) == 0
        a = pltpu.roll(pltpu.roll(v, 8 - step, 0), 16 * step, 1)
        b = a if k == 2 else pltpu.roll(pltpu.roll(v, step, 0), 128 - 16 * step, 1)
        v = jnp.where(up == left, v, jnp.where(up, a, b))
    return v


def kernel(
    inter, og, tw, pooled, bags, place,
    w_out, t_out,
    prod, sym, rs_buf, rx_buf, gg, cf, pf, pl_buf, iota_buf, cnt,
    ig, wt, wx, ws, wr, wf, wxh,
    td, tx, ts, tr, tf, txh,
    rs_s, rs_r, rx_s, rx_r, gg_s, gg_r, gp_s, gp_r, ig_s, ig_r, ip_s, ip_r,
    wx_s, wx_r, wy_s, wy_r, wh_s, wh_r, tx_s, tx_r, ty_s, ty_r, th_s, th_r,
    loc_s,
):
    col, smp = lax.axis_index("col"), lax.axis_index("sample")
    z, x = col // NX, col % NX
    xh, y, core = smp // 16, (smp // 2) % NY, smp % 2

    def col_dev(zz, xx):
        return {"col": zz * NX + xx, "sample": smp}

    def smp_dev(hh, yy, cc):
        return {"col": col, "sample": hh * 16 + yy * 2 + cc}

    zdev = [col_dev((z + 1) % NZ, x), col_dev((z + NZ - 1) % NZ, x)]
    xdev = col_dev(z, 1 - x)
    cdev = smp_dev(xh, y, 1 - core)
    hdev = smp_dev(1 - xh, y, core)

    def ydev(o):
        return smp_dev(xh, (y + o) % NY, core)

    def rc(src, dst, ss, rs, dev):
        return pltpu.make_async_remote_copy(
            src_ref=src, dst_ref=dst, send_sem=ss, recv_sem=rs, device_id=dev, device_id_type=MESH
        )

    barrier = pltpu.get_barrier_semaphore()
    friends = zdev + [xdev, cdev, hdev] + [ydev(o) for o in range(1, NY)]
    for dev in friends:
        pl.semaphore_signal(barrier, inc=1, device_id=dev, device_id_type=MESH)

    own = pltpu.make_async_copy(inter, ig.at[z, x], loc_s.at[0])
    own.start()

    for l in range(L):
        slot = bags[:, l, :]
        for h in range(2):
            ids = slot[:, h * 128:(h + 1) * 128]
            low, high = ids & 127, ids >> 7
            got = jnp.zeros((F, 128), I32)
            for k in range(4):
                part = jnp.take_along_axis(place[:, k * 128:(k + 1) * 128], low, axis=1, mode="promise_in_bounds")
                got = jnp.where(high == k, part, got)
            got = (got & 0xEF) | (((got >> 8) & 1) << 4) | (((got >> 4) & 1) << 8)
            pl_buf[l * F:(l + 1) * F, h * 128:(h + 1) * 128] = (got - 256).astype(F32)
    iota_buf[...] = (lax.broadcasted_iota(I32, (RT, SB), 0) - 256).astype(F32).astype(BF16)

    own.wait()
    pl.semaphore_wait(barrier, len(friends))

    class Gather:
        def __init__(self, buf, s, r, ps, pr):
            self.buf, self.s, self.r, self.ps, self.pr = buf, s, r, ps, pr

        def part(self, i):
            return x if i == 0 else 1 - x

        def copy(self, i, d, k):
            zz = (z + NZ - k) % NZ if d == 0 else (z + k) % NZ
            at = self.buf.at[zz, self.part(i)]
            return rc(at, at, self.s.at[i, d, k], self.r.at[i, d, k], zdev[d])

        def arrival(self, i, d, k):
            zz = (z + NZ - k - 1) % NZ if d == 0 else (z + k + 1) % NZ
            at = self.buf.at[zz, self.part(i)]
            return rc(at, at, self.s.at[i, d, k], self.r.at[i, d, k], zdev[d])

        def pair(self):
            at = self.buf.at[z, x]
            return rc(at, at, self.ps.at[0], self.pr.at[0], xdev)

        def has(self, i, d, k):
            return k < 3 or (k == 3 and i == d)

        def start0(self):
            for d in range(2):
                self.copy(0, d, 0).start()
            self.pair().start()

        def start1(self):
            at = self.buf.at[z, 1 - x]
            rc(at, at, self.ps.at[0], self.pr.at[0], xdev).wait_recv()
            for d in range(2):
                self.copy(1, d, 0).start()

        def hop(self, k):
            for i in range(2):
                for d in range(2):
                    if self.has(i, d, k - 1):
                        self.arrival(i, d, k - 1).wait_recv()
                    if self.has(i, d, k):
                        self.copy(i, d, k).start()

        def end(self):
            self.hop(4)

        def drain(self):
            self.pair().wait_send()
            for i in range(2):
                for d in range(2):
                    for k in range(4):
                        if self.has(i, d, k):
                            self.copy(i, d, k).wait_send()

    g_inter = Gather(ig, ig_s, ig_r, ip_s, ip_r)
    g_gram = Gather(gg, gg_s, gg_r, gp_s, gp_r)
    g_inter.start0()

    for b in range(6):
        r = lax.dot_general(tw[b * 384:(b + 1) * 384, :], og[...], NT, preferred_element_type=F32)
        for ii in range(8):
            i = b * 8 + ii
            blk = r[ii * F:(ii + 1) * F]
            for row in (i, i + F):
                if row < EXT:
                    for h in range(2):
                        half = blk[:, h * 128:(h + 1) * 128]
                        prod[h, row * EXT:row * EXT + F, :] = half
                        prod[h, row * EXT + F:(row + 1) * EXT, :] = half[:F // 2]
    for d in range(OFF):
        for h in range(2):
            both = prod[h, pl.ds(d, F, stride=EXT + 1), :] + prod[h, pl.ds(EXT * d, F, stride=EXT + 1), :]
            for m in range(3):
                at = d * F + 16 * m
                c, r0 = at // CH, at % CH
                sym[c // NX, c % NX, r0:r0 + 16, h * 128:(h + 1) * 128] = both[16 * m:16 * (m + 1)]
    sym[NZ - 1, NX - 1] = jnp.zeros((CH, SB), F32)

    def rs_copy(d, k):
        t = (z + 4 - k) % NZ if d == 0 else (z + 4 + k) % NZ
        if k == 0:
            return rc(sym.at[t, d], rs_buf.at[d, k, d], rs_s.at[d, k], rs_r.at[d, k], zdev[d])
        return rc(sym.at[t], rs_buf.at[d, k], rs_s.at[d, k], rs_r.at[d, k], zdev[d])

    def rs_step(k):
        for d in range(2):
            if k > 0:
                rs_copy(d, k - 1).wait_recv()
                t = (z + 4 - k) % NZ if d == 0 else (z + 4 + k) % NZ
                if k == 1:
                    sym[t, d] = sym[t, d] + rs_buf[d, 0, d]
                else:
                    sym[t] = sym[t] + rs_buf[d, k - 1]
            if k < 4:
                rs_copy(d, k).start()

    def count(f, carry):
        rows = [pl_buf[pl.ds(l * F + f, 1), :].astype(BF16) for l in range(L)]
        for ch in range(4):
            io = iota_buf[ch * 128:(ch + 1) * 128, :]
            acc = jnp.zeros((128, SB), BF16)
            for l in range(L):
                acc = acc + jnp.where(io == rows[l], jnp.ones((), BF16), jnp.zeros((), BF16))
            cnt[f, ch * 128:(ch + 1) * 128, :] = acc
        return carry

    def counts(lo, hi):
        lax.fori_loop(lo, hi, count, 0)

    rs_step(0)
    counts(0, 4)
    g_inter.start1()
    rs_step(1)
    counts(4, 12)
    rs_step(2)
    g_inter.hop(1)
    counts(12, 20)
    rs_step(3)
    g_inter.hop(2)
    counts(20, 28)
    rs_step(4)
    rxc = rc(sym.at[z, 1 - x], rx_buf, rx_s.at[0], rx_r.at[0], xdev)
    rxc.start()
    g_inter.hop(3)
    for j in range(F):
        v = pooled[j].astype(F32)
        pf[j] = v
        pf[j + F] = v
    rxc.wait_recv()
    gg[z, x] = (sym[z, x] + rx_buf[...]).astype(BF16)
    g_gram.start0()
    counts(28, 34)
    g_gram.start1()
    g_inter.end()
    g_gram.hop(1)

    def w_copy(cb):
        return rc(wt.at[cb, 1 - core], wx.at[cb], wx_s.at[cb], wx_r.at[cb], cdev)

    for zz in range(NZ):
        r = jnp.dot(ig[zz].reshape(2 * IR, SB), og[...], preferred_element_type=F32)
        for q in range(2):
            for cc in range(2):
                wt[zz * 2 + q, cc] = r[q * IR + cc * WR:q * IR + (cc + 1) * WR]
            w_copy(zz * 2 + q).start()
        if zz == 3:
            g_gram.hop(2)
    g_gram.hop(3)

    def wy_copy(o):
        return rc(ws.at[(y + o) % NY], wr.at[o], wy_s.at[o], wy_r.at[o], ydev(o))

    for o in range(NY):
        yy = (y + o) % NY
        for h in range(2):
            cb = h * NY + yy
            w_copy(cb).wait_recv()
            v = wt[cb, core] + wx[cb]
            ws[yy, h] = jnp.concatenate([v[:, :128], v[:, 128:]], axis=0).astype(BF16)
        if o > 0:
            wy_copy(o).start()
    counts(34, F)
    g_gram.end()

    for at in range(0, OFF * F, 16):
        c, r0 = at // CH, at % CH
        v = gg[c // NX, c % NX, r0:r0 + 16, :].astype(F32)
        d, i0 = at // F, at % F
        for base in (d * 2 * F + i0, d * 2 * F + F + i0):
            cf[base:base + 16, :] = v

    rows8 = lax.broadcasted_iota(I32, (8, 128), 0)
    lanes8 = lax.broadcasted_iota(I32, (8, 128), 1)

    def pooled_grad(i):
        accs = [jnp.zeros((E8, SB), F32) for _ in range(4)]
        n = 0
        for d in range(OFF):
            accs[n % 4] = accs[n % 4] + cf[pl.ds(i + d * 2 * F, 1), :] * pf[i + d]
            n += 1
        for d in range(1, OFF - 1):
            accs[n % 4] = accs[n % 4] + cf[pl.ds(i + (d * 2 * F + F - d), 1), :] * pf[i + (F - d)]
            n += 1
        v = (accs[0] + accs[1]) + (accs[2] + accs[3])
        hi = v.astype(BF16)
        lo = (v - hi.astype(F32)).astype(BF16)
        return jnp.concatenate([hi, lo], axis=0)

    def table_rows(f, fl, g, halves):
        r = lax.dot_general(halves, cnt[f], NT, preferred_element_type=F32)
        r = r[:E8] + r[E8:]
        for k in range(4):
            v = swap_groups(r[:, k * 128:(k + 1) * 128], rows8, lanes8)
            td[g, k // 2, pl.ds((k % 2) * 128 + fl, 8, stride=GF), :] = v

    def tx_copy(g):
        return rc(td.at[g, 1 - core], tx.at[g], tx_s.at[g], tx_r.at[g], cdev)

    def ty_copy(g, o):
        return rc(ts.at[g, (y + o) % NY], tr.at[g, o], ty_s.at[g, o], ty_r.at[g, o], ydev(o))

    def t_send(g):
        tx_copy(g).wait_recv()
        v = td[g, core] + tx[g]
        ts[g] = v.astype(BF16).reshape(NY, 2 * GF, 128)
        for o in range(1, NY):
            ty_copy(g, o).start()

    for g in range(NG):
        def body(fl, carry, g=g):
            table_rows(g * GF + fl, fl, g, pooled_grad(g * GF + fl))
            return carry

        lax.fori_loop(0, GF, body, 0)
        tx_copy(g).start()
        if g > 0:
            t_send(g - 1)
    t_send(NG - 1)

    wtot = ws[y].astype(F32)
    for o in range(1, NY):
        wy_copy(o).wait_recv()
        wtot = wtot + wr[o].astype(F32)
    wf[...] = wtot
    ws[y] = wtot.astype(BF16)
    whc = rc(ws.at[y, 1 - xh], wxh, wh_s.at[0], wh_r.at[0], hdev)
    whc.start()
    for g in range(NG):
        tot = ts[g, y].astype(F32)
        for o in range(1, NY):
            ty_copy(g, o).wait_recv()
            tot = tot + tr[g, o].astype(F32)
        tf[g] = tot.reshape(2, GF, 128)
    thc = rc(tf.at[:, 1 - xh], txh, th_s.at[0], th_r.at[0], hdev)
    thc.start()
    whc.wait_recv()
    tot = wf[xh] + wxh[...].astype(F32)
    w_out[:, :128] = tot[:WR]
    w_out[:, 128:] = tot[WR:]
    thc.wait_recv()
    for g in range(NG):
        tot = tf[g, xh] + txh[g]
        for e in range(E8):
            t_out[e, g * GF:(g + 1) * GF, :] = tot[:, e * 16:(e + 1) * 16]

    for d in range(2):
        for k in range(4):
            rs_copy(d, k).wait_send()
    rxc.wait_send()
    g_inter.drain()
    g_gram.drain()
    for cb in range(16):
        w_copy(cb).wait_send()
    for o in range(1, NY):
        wy_copy(o).wait_send()
    whc.wait_send()
    for g in range(NG):
        tx_copy(g).wait_send()
        for o in range(1, NY):
            ty_copy(g, o).wait_send()
    thc.wait_send()


def shards(interaction, out_grad, top_weight, pooled, bags, row_place):
    dma = pltpu.SemaphoreType.DMA
    v = pltpu.VMEM
    vmem = pl.BlockSpec(memory_space=pltpu.VMEM)
    gather_sems = [dma((2, 2, 4)), dma((2, 2, 4)), dma((1,)), dma((1,))]
    return pl.pallas_call(
        kernel,
        out_shape=(
            jax.ShapeDtypeStruct((WR, HB), F32),
            jax.ShapeDtypeStruct((E8, F, 16), F32),
        ),
        in_specs=[vmem] * 6,
        out_specs=(vmem, vmem),
        scratch_shapes=[
            v((2, EXT * EXT, 128), F32),
            v((NZ, NX, CH, SB), F32),
            v((2, 4, NX, CH, SB), F32),
            v((CH, SB), F32),
            v((NZ, NX, CH, SB), BF16),
            v((OFF * 2 * F, SB), F32),
            v((2 * F, E8, SB), F32),
            v((L * F, SB), F32),
            v((RT, SB), BF16),
            v((F, RT, SB), BF16),
            v((NZ, NX, IR, SB), BF16),
            v((16, 2, WR, HB), F32),
            v((16, WR, HB), F32),
            v((NY, 2, 2 * WR, 128), BF16),
            v((NY, 2, 2 * WR, 128), BF16),
            v((2, 2 * WR, 128), F32),
            v((2 * WR, 128), BF16),
            v((NG, 2, 16 * GF, 128), F32),
            v((NG, 16 * GF, 128), F32),
            v((NG, NY, 2 * GF, 128), BF16),
            v((NG, NY, 2 * GF, 128), BF16),
            v((NG, 2, GF, 128), F32),
            v((NG, GF, 128), F32),
            dma((2, 4)), dma((2, 4)), dma((1,)), dma((1,)),
            *gather_sems, *gather_sems,
            dma((16,)), dma((16,)), dma((NY,)), dma((NY,)), dma((1,)), dma((1,)),
            dma((NG,)), dma((NG,)), dma((NG, NY)), dma((NG, NY)), dma((1,)), dma((1,)),
            dma((1,)),
        ],
        compiler_params=pltpu.CompilerParams(
            collective_id=0, has_side_effects=True, vmem_limit_bytes=56 * 1024 * 1024
        ),
    )(interaction, out_grad, top_weight, pooled, bags, row_place)


def solution(mesh):
    in_specs = (
        P("col", "sample"),
        P("sample", "col"),
        P(None, "col"),
        P(None, "col", "sample"),
        P(None, None, "sample"),
        P(),
    )
    out_specs = (P("sample", "col"), P("col", None, "sample"))
    return jax.shard_map(shards, mesh=mesh, in_specs=in_specs, out_specs=out_specs, check_vma=False)
```

```python
import jax
import jax.numpy as jnp
from jax import lax
from jax.experimental import pallas as pl
from jax.experimental.pallas import tpu as pltpu
from jax.sharding import PartitionSpec as P

MESH = pl.DeviceIdType.MESH
F32, BF16, I32 = jnp.float32, jnp.bfloat16, jnp.int32

F, E8, SB, HB, L, RT = 48, 8, 256, 256, 4, 512
NZ, NX, NY = 8, 2, 8
OFF = F // 2 + 1
CH = 80
RA, RB = 32, 48
WR = 72
IR = 144
GF = 16
NG = F // GF
EXT = F + F // 2
NT = (((1,), (1,)), ((), ()))


def take(v, at, axis):
    return jnp.take_along_axis(v, at, axis=axis, mode="promise_in_bounds")


def kernel(
    inter_hbm, og_hbm, tw_hbm, pooled_hbm, bags_hbm, place_hbm,
    w_out, t_out,
    og, tw, pooled, bags, place,
    prod, sym, ra_buf, rb_buf, bx_buf, rx_buf, gg, cf, pf, pl_buf, iota_buf, cnt,
    ig, wt, wx, ws, wr, wf, wxh,
    td, tx, ts, tr, tf, txh,
    ra_s, ra_r, rb_s, rb_r, bx_s, bx_r, rx_s, rx_r,
    ga_s, ga_r, gx_s, gx_r, gb_s, gb_r, gp_s, gp_r,
    ia_s, ia_r, ix_s, ix_r, ib_s, ib_r, ip_s, ip_r,
    wx_s, wx_r, wy_s, wy_r, wh_s, wh_r, tx_s, tx_r, ty_s, ty_r, th_s, th_r,
    loc_s,
):
    col, smp = lax.axis_index("col"), lax.axis_index("sample")
    z, x = col // NX, col % NX
    xh, y, core = smp // 16, (smp // 2) % NY, smp % 2

    def col_dev(zz, xx):
        return {"col": zz * NX + xx, "sample": smp}

    def smp_dev(hh, yy, cc):
        return {"col": col, "sample": hh * 16 + yy * 2 + cc}

    zdev = [col_dev((z + 1) % NZ, x), col_dev((z + NZ - 1) % NZ, x)]
    xdev = col_dev(z, 1 - x)
    cdev = smp_dev(xh, y, 1 - core)
    hdev = smp_dev(1 - xh, y, core)

    def ydev(o):
        return smp_dev(xh, (y + o) % NY, core)

    sent = []

    class Copy:
        def __init__(self, src, dst, sems, at, dev):
            self.key = (id(sems[1]), at)
            self.copy = pltpu.make_async_remote_copy(
                src_ref=src, dst_ref=dst, send_sem=sems[0].at[at], recv_sem=sems[1].at[at],
                device_id=dev, device_id_type=MESH,
            )

        def start(self):
            self.copy.start()
            sent.append(self)

        def wait_recv(self):
            self.copy.wait_recv()

    def rc(src, dst, sems, at, dev):
        return Copy(src, dst, sems, at, dev)

    barrier = pltpu.get_barrier_semaphore()
    friends = zdev + [xdev, cdev, hdev] + [ydev(o) for o in range(1, NY)]
    for dev in friends:
        pl.semaphore_signal(barrier, inc=1, device_id=dev, device_id_type=MESH)

    loads = [
        pltpu.make_async_copy(src, dst, loc_s.at[n])
        for n, (src, dst) in enumerate(
            ((inter_hbm, ig.at[z, x]), (og_hbm, og), (tw_hbm, tw), (pooled_hbm, pooled), (bags_hbm, bags), (place_hbm, place))
        )
    ]
    for load in loads:
        load.start()
    loads[0].wait()
    pl.semaphore_wait(barrier, len(friends))

    def find_places():
        for l in range(L):
            slot = bags[:, l, :]
            for h in range(2):
                ids = slot[:, h * 128:(h + 1) * 128]
                low, high = ids & 127, ids >> 7
                got = jnp.zeros((F, 128), I32)
                for k in range(4):
                    part = take(place[:, k * 128:(k + 1) * 128], low, 1)
                    got = jnp.where(high == k, part, got)
                got = (got & 0xEF) | (((got >> 8) & 1) << 4) | (((got >> 4) & 1) << 8)
                pl_buf[l * F:(l + 1) * F, h * 128:(h + 1) * 128] = (got - 256).astype(F32)
        iota_buf[...] = (lax.broadcasted_iota(I32, (RT, SB), 0) - 256).astype(F32).astype(BF16)

    class Gather:
        def __init__(self, buf, cut, half, za, xa, zb, xb):
            self.buf, self.cut, self.half, self.rows = buf, cut, half, buf.shape[2]
            self.za, self.xa, self.zb, self.xb = za, xa, zb, xb

        def first(self, d, k, held):
            m = (NZ - k if d == 0 else k) if held else (NZ - k - 1 if d == 0 else k + 1)
            lo, hi = (0, self.cut) if k < 3 else ((0, self.half), (self.half, self.cut))[d]
            at = self.buf.at[(z + m) % NZ, x, pl.ds(lo, hi - lo)]
            return rc(at, at, self.za, (d, k), zdev[d])

        def across(self, m, xx):
            at = self.buf.at[(z + m) % NZ, xx, pl.ds(0, self.cut)]
            return rc(at, at, self.xa, (m % NZ,), xdev)

        def second(self, i, d, k, held):
            m = (NZ - k if d == 0 else k) if held else (NZ - k - 1 if d == 0 else k + 1)
            at = self.buf.at[(z + m) % NZ, x if i == 0 else 1 - x, pl.ds(self.cut, self.rows - self.cut)]
            return rc(at, at, self.zb, (i, d, k), zdev[d])

        def pair(self, xx):
            at = self.buf.at[z, xx, pl.ds(self.cut, self.rows - self.cut)]
            return rc(at, at, self.xb, (0,), xdev)

        def has(self, i, d, k):
            return k < 3 or (k == 3 and i == d)

        def start(self):
            self.pair(x).start()
            for d in range(2):
                self.first(d, 0, True).start()
            for d in range(2):
                self.second(0, d, 0, True).start()
            self.across(0, x).start()

        def start_pair(self):
            self.pair(1 - x).wait_recv()
            for d in range(2):
                self.second(1, d, 0, True).start()

        def hop_first(self, k):
            for d in range(2):
                self.first(d, k - 1, False).wait_recv()
                if k < 4:
                    self.first(d, k, True).start()
                    self.across(NZ - k if d == 0 else k, x).start()
            if k == 4:
                self.across(4, x).start()

        def hop_second(self, k):
            for i in range(2):
                for d in range(2):
                    if self.has(i, d, k - 1):
                        self.second(i, d, k - 1, False).wait_recv()
                    if self.has(i, d, k):
                        self.second(i, d, k, True).start()

        def end(self):
            for m in range(NZ):
                self.across(m, 1 - x).wait_recv()

    g_inter = Gather(ig, 80, 48, (ia_s, ia_r), (ix_s, ix_r), (ib_s, ib_r), (ip_s, ip_r))
    g_gram = Gather(gg, 48, 32, (ga_s, ga_r), (gx_s, gx_r), (gb_s, gb_r), (gp_s, gp_r))
    g_inter.start()
    loads[1].wait()
    loads[2].wait()

    for b in range(6):
        r = lax.dot_general(tw[b * 384:(b + 1) * 384, :], og[...], NT, preferred_element_type=F32)
        for ii in range(8):
            i = b * 8 + ii
            blk = r[ii * F:(ii + 1) * F]
            for row in (i, i + F):
                if row < EXT:
                    for h in range(2):
                        half = blk[:, h * 128:(h + 1) * 128]
                        prod[h, row * EXT:row * EXT + F, :] = half
                        prod[h, row * EXT + F:(row + 1) * EXT, :] = half[:F // 2]
    for d in range(OFF):
        for h in range(2):
            both = prod[h, pl.ds(d, F, stride=EXT + 1), :] + prod[h, pl.ds(EXT * d, F, stride=EXT + 1), :]
            for m in range(3):
                at = d * F + 16 * m
                c, r0 = at // CH, at % CH
                sym[c // NX, c % NX, r0:r0 + 16, h * 128:(h + 1) * 128] = both[16 * m:16 * (m + 1)]
    sym[NZ - 1, NX - 1] = jnp.zeros((CH, SB), F32)

    def dest(d, k):
        return (z + 4 - k) % NZ if d == 0 else (z + 4 + k) % NZ

    def ra_copy(d, k):
        if k == 0:
            return rc(sym.at[dest(d, k), d, pl.ds(0, RA)], ra_buf.at[d, k, d], (ra_s, ra_r), (d, k), zdev[d])
        return rc(sym.at[dest(d, k), :, pl.ds(0, RA)], ra_buf.at[d, k], (ra_s, ra_r), (d, k), zdev[d])

    def ra_step(k):
        for d in range(2):
            if k > 0:
                ra_copy(d, k - 1).wait_recv()
                t = dest(d, k)
                if k == 1:
                    sym[t, d, :RA, :] = sym[t, d, :RA, :] + ra_buf[d, 0, d]
                else:
                    sym[t, :, :RA, :] = sym[t, :, :RA, :] + ra_buf[d, k - 1]
            if k < 4:
                ra_copy(d, k).start()

    def ra_swap():
        return rc(sym.at[z, 1 - x, pl.ds(0, RA)], rx_buf, (rx_s, rx_r), (0,), xdev)

    def bx_copy(m):
        return rc(sym.at[(z + m) % NZ, 1 - x, pl.ds(RA, RB)], bx_buf.at[m], (bx_s, bx_r), (m,), xdev)

    def bx_add(m):
        bx_copy(m).wait_recv()
        t = (z + m) % NZ
        sym[t, x, RA:, :] = sym[t, x, RA:, :] + bx_buf[m]

    def rb_copy(d, k):
        if k == 0:
            part = pl.ds(d * (RB // 2), RB // 2)
            return rc(sym.at[dest(d, k), x, pl.ds(RA + d * (RB // 2), RB // 2)], rb_buf.at[d, k, part], (rb_s, rb_r), (d, k), zdev[d])
        return rc(sym.at[dest(d, k), x, pl.ds(RA, RB)], rb_buf.at[d, k], (rb_s, rb_r), (d, k), zdev[d])

    def rb_step(k):
        if k == 0:
            bx_add(4)
        elif k < 4:
            bx_add(4 - k)
            bx_add(4 + k)
        else:
            bx_add(0)
        for d in range(2):
            if k > 0:
                rb_copy(d, k - 1).wait_recv()
                t = dest(d, k)
                if k == 1:
                    lo = d * (RB // 2)
                    hi = lo + RB // 2
                    sym[t, x, RA + lo:RA + hi, :] = sym[t, x, RA + lo:RA + hi, :] + rb_buf[d, 0, lo:hi, :]
                else:
                    sym[t, x, RA:, :] = sym[t, x, RA:, :] + rb_buf[d, k - 1]
            if k < 4:
                rb_copy(d, k).start()

    def count(f, carry):
        rows = [pl_buf[pl.ds(l * F + f, 1), :].astype(BF16) for l in range(L)]
        for ch in range(4):
            io = iota_buf[ch * 128:(ch + 1) * 128, :]
            acc = jnp.zeros((128, SB), BF16)
            for l in range(L):
                acc = acc + jnp.where(io == rows[l], jnp.ones((), BF16), jnp.zeros((), BF16))
            cnt[f, ch * 128:(ch + 1) * 128, :] = acc
        return carry

    def counts(lo, hi):
        lax.fori_loop(lo, hi, count, 0)

    ra_step(0)
    for m in (4, 3, 5, 2, 6, 1, 7, 0):
        bx_copy(m).start()
    for n in (3, 4, 5):
        loads[n].wait()
    find_places()
    g_inter.start_pair()
    counts(0, 4)
    ra_step(1)
    g_inter.hop_first(1)
    g_inter.hop_second(1)
    counts(4, 10)
    ra_step(2)
    rb_step(0)
    g_inter.hop_first(2)
    g_inter.hop_second(2)
    counts(10, 16)
    ra_step(3)
    rb_step(1)
    g_inter.hop_first(3)
    g_inter.hop_second(3)
    counts(16, 22)
    ra_step(4)
    ra_swap().start()
    rb_step(2)
    g_inter.hop_first(4)
    g_inter.hop_second(4)
    for j in range(F):
        v = pooled[j].astype(F32)
        pf[j] = v
        pf[j + F] = v
    rb_step(3)
    counts(22, 28)
    rb_step(4)
    ra_swap().wait_recv()
    gg[z, x, :RA, :] = (sym[z, x, :RA, :] + rx_buf[...]).astype(BF16)
    gg[z, x, RA:, :] = sym[z, x, RA:, :].astype(BF16)
    g_gram.start()
    g_inter.end()

    def w_copy(cb):
        return rc(wt.at[cb, 1 - core], wx.at[cb], (wx_s, wx_r), (cb,), cdev)

    for zz in range(NZ):
        r = jnp.dot(ig[zz].reshape(2 * IR, SB), og[...], preferred_element_type=F32)
        for q in range(2):
            for cc in range(2):
                wt[zz * 2 + q, cc] = r[q * IR + cc * WR:q * IR + (cc + 1) * WR]
            w_copy(zz * 2 + q).start()
        if zz == 2:
            g_gram.start_pair()
        if zz == 5:
            g_gram.hop_first(1)
            g_gram.hop_second(1)
    g_gram.hop_first(2)
    g_gram.hop_second(2)

    def wy_copy(o):
        return rc(ws.at[(y + o) % NY], wr.at[o], (wy_s, wy_r), (o,), ydev(o))

    for o in range(NY):
        yy = (y + o) % NY
        for h in range(2):
            cb = h * NY + yy
            w_copy(cb).wait_recv()
            v = wt[cb, core] + wx[cb]
            ws[yy, h] = jnp.concatenate([v[:, :128], v[:, 128:]], axis=0).astype(BF16)
        if o > 0:
            wy_copy(o).start()
        if o == 3:
            g_gram.hop_first(3)
            g_gram.hop_second(3)
    counts(28, F)
    g_gram.hop_first(4)
    g_gram.hop_second(4)
    g_gram.end()

    for at in range(0, OFF * F, 16):
        c, r0 = at // CH, at % CH
        v = gg[c // NX, c % NX, r0:r0 + 16, :].astype(F32)
        d, i0 = at // F, at % F
        for base in (d * 2 * F + i0, d * 2 * F + F + i0):
            cf[base:base + 16, :] = v

    row = lax.broadcasted_iota(I32, (8, 128), 0)
    lane = lax.broadcasted_iota(I32, (8, 128), 1)
    grp, low4 = lane >> 4, lane & 15
    turn_a = (((grp + row) & 7) << 4) | low4
    turn_b = (row - grp) & 7
    turn_c = (((row - grp) & 7) << 4) | low4

    def pooled_grad(i):
        accs = [jnp.zeros((E8, SB), F32) for _ in range(4)]
        n = 0
        for d in range(OFF):
            accs[n % 4] = accs[n % 4] + cf[pl.ds(i + d * 2 * F, 1), :] * pf[i + d]
            n += 1
        for d in range(1, OFF - 1):
            accs[n % 4] = accs[n % 4] + cf[pl.ds(i + (d * 2 * F + F - d), 1), :] * pf[i + (F - d)]
            n += 1
        v = (accs[0] + accs[1]) + (accs[2] + accs[3])
        hi = v.astype(BF16)
        lo = (v - hi.astype(F32)).astype(BF16)
        return jnp.concatenate([hi, lo], axis=0)

    def table_rows(f, fl, g, halves):
        r = lax.dot_general(halves, cnt[f], NT, preferred_element_type=F32)
        r = r[:E8] + r[E8:]
        for k in range(4):
            v = take(take(take(r[:, k * 128:(k + 1) * 128], turn_a, 1), turn_b, 0), turn_c, 1)
            td[g, k // 2, pl.ds((k % 2) * 128 + fl, 8, stride=GF), :] = v

    def tx_copy(g):
        return rc(td.at[g, 1 - core], tx.at[g], (tx_s, tx_r), (g,), cdev)

    def ty_copy(g, o):
        return rc(ts.at[g, (y + o) % NY], tr.at[g, o], (ty_s, ty_r), (g, o), ydev(o))

    def t_send(g):
        tx_copy(g).wait_recv()
        v = td[g, core] + tx[g]
        ts[g] = v.astype(BF16).reshape(NY, 2 * GF, 128)
        for o in range(1, NY):
            ty_copy(g, o).start()

    halves = pooled_grad(0)
    for g in range(NG):
        def body(fl, halves, g=g):
            table_rows(g * GF + fl, fl, g, halves)
            return pooled_grad(g * GF + fl + 1)

        halves = lax.fori_loop(0, GF, body, halves, unroll=GF)
        tx_copy(g).start()
        if g > 0:
            t_send(g - 1)
    t_send(NG - 1)

    wtot = ws[y].astype(F32)
    for o in range(1, NY):
        wy_copy(o).wait_recv()
        wtot = wtot + wr[o].astype(F32)
    wf[...] = wtot
    ws[y] = wtot.astype(BF16)
    whc = rc(ws.at[y, 1 - xh], wxh, (wh_s, wh_r), (0,), hdev)
    whc.start()
    for g in range(NG):
        tot = ts[g, y].astype(F32)
        for o in range(1, NY):
            ty_copy(g, o).wait_recv()
            tot = tot + tr[g, o].astype(F32)
        tf[g] = tot.reshape(2, GF, 128)
    thc = rc(tf.at[:, 1 - xh], txh, (th_s, th_r), (0,), hdev)
    thc.start()
    whc.wait_recv()
    tot = wf[xh] + wxh[...].astype(F32)
    w_out[:, :128] = tot[:WR]
    w_out[:, 128:] = tot[WR:]
    thc.wait_recv()
    for g in range(NG):
        tot = tf[g, xh] + txh[g]
        for e in range(E8):
            t_out[e, g * GF:(g + 1) * GF, :] = tot[:, e * 16:(e + 1) * 16]

    for copy in sent:
        copy.copy.wait_send()


def shards(interaction, out_grad, top_weight, pooled, bags, row_place):
    dma = pltpu.SemaphoreType.DMA
    v = pltpu.VMEM
    vmem = pl.BlockSpec(memory_space=pltpu.VMEM)
    gather_sems = [dma(n) for n in ((2, 4), (NZ,), (2, 2, 4), (1,)) for _ in range(2)]
    return pl.pallas_call(
        kernel,
        out_shape=(
            jax.ShapeDtypeStruct((WR, HB), F32),
            jax.ShapeDtypeStruct((E8, F, 16), F32),
        ),
        in_specs=[pl.BlockSpec(memory_space=pl.ANY)] * 6,
        out_specs=(vmem, vmem),
        scratch_shapes=[
            v((SB, HB), BF16), v((F * F, HB), BF16), v((F, E8, SB), BF16), v((F, L, SB), I32), v((F, RT), I32),
            v((2, EXT * EXT, 128), F32),
            v((NZ, NX, CH, SB), F32),
            v((2, 4, NX, RA, SB), F32),
            v((2, 4, RB, SB), F32),
            v((NZ, RB, SB), F32),
            v((RA, SB), F32),
            v((NZ, NX, CH, SB), BF16),
            v((OFF * 2 * F, SB), F32),
            v((2 * F, E8, SB), F32),
            v((L * F, SB), F32),
            v((RT, SB), BF16),
            v((F, RT, SB), BF16),
            v((NZ, NX, IR, SB), BF16),
            v((16, 2, WR, HB), F32),
            v((16, WR, HB), F32),
            v((NY, 2, 2 * WR, 128), BF16),
            v((NY, 2, 2 * WR, 128), BF16),
            v((2, 2 * WR, 128), F32),
            v((2 * WR, 128), BF16),
            v((NG, 2, 16 * GF, 128), F32),
            v((NG, 16 * GF, 128), F32),
            v((NG, NY, 2 * GF, 128), BF16),
            v((NG, NY, 2 * GF, 128), BF16),
            v((NG, 2, GF, 128), F32),
            v((NG, GF, 128), F32),
            dma((2, 4)), dma((2, 4)), dma((2, 4)), dma((2, 4)), dma((NZ,)), dma((NZ,)), dma((1,)), dma((1,)),
            *gather_sems, *gather_sems,
            dma((16,)), dma((16,)), dma((NY,)), dma((NY,)), dma((1,)), dma((1,)),
            dma((NG,)), dma((NG,)), dma((NG, NY)), dma((NG, NY)), dma((1,)), dma((1,)),
            dma((6,)),
        ],
        compiler_params=pltpu.CompilerParams(
            collective_id=0, has_side_effects=True, vmem_limit_bytes=56 * 1024 * 1024
        ),
    )(interaction, out_grad, top_weight, pooled, bags, row_place)


def solution(mesh):
    in_specs = (
        P("col", "sample"),
        P("sample", "col"),
        P(None, "col"),
        P(None, "col", "sample"),
        P(None, None, "sample"),
        P(),
    )
    out_specs = (P("sample", "col"), P("col", None, "sample"))
    return jax.shard_map(shards, mesh=mesh, in_specs=in_specs, out_specs=out_specs, check_vma=False)
```

```python
import jax
import jax.numpy as jnp
from jax import lax
from jax.experimental import pallas as pl
from jax.experimental.pallas import tpu as pltpu
from jax.sharding import PartitionSpec as P

MESH = pl.DeviceIdType.MESH
F32, BF16, I32 = jnp.float32, jnp.bfloat16, jnp.int32

F, E8, SB, HB, L, RT = 48, 8, 256, 256, 4, 512
NZ, NX, NY = 8, 2, 8
OFF = F // 2 + 1
CH = 80
RA, RB = 32, 48
WR = 72
IR = 144
GF = 16
NG = F // GF
EXT = F + F // 2
NT = (((1,), (1,)), ((), ()))


def take(v, at, axis):
    return jnp.take_along_axis(v, at, axis=axis, mode="promise_in_bounds")


def kernel(
    inter_hbm, og_hbm, tw_hbm, pooled_hbm, bags_hbm, place_hbm,
    w_out, t_out,
    og, tw, pooled, bags, place,
    prod, sym, ra_buf, rb_buf, bx_buf, rx_buf, gg, cf, pf, pl_buf, iota_buf, cnt,
    ig, wt, wx, ws, wr, wf, wxh,
    td, tx, ts, tr,
    ra_s, ra_r, rb_s, rb_r, bx_s, bx_r, rx_s, rx_r,
    ga_s, ga_r, gx_s, gx_r, gb_s, gb_r, gp_s, gp_r,
    ia_s, ia_r, ix_s, ix_r, ib_s, ib_r, ip_s, ip_r,
    wx_s, wx_r, wy_s, wy_r, wh_s, wh_r, tx_s, tx_r, ty_s, ty_r,
    loc_s,
):
    col, smp = lax.axis_index("col"), lax.axis_index("sample")
    z, x = col // NX, col % NX
    xh, y, core = smp // 16, (smp // 2) % NY, smp % 2

    def col_dev(zz, xx):
        return {"col": zz * NX + xx, "sample": smp}

    def smp_dev(hh, yy, cc):
        return {"col": col, "sample": hh * 16 + yy * 2 + cc}

    zdev = [col_dev((z + 1) % NZ, x), col_dev((z + NZ - 1) % NZ, x)]
    zdev2 = [col_dev((z + 2) % NZ, x), col_dev((z + NZ - 2) % NZ, x)]
    xdev = col_dev(z, 1 - x)
    cdev = smp_dev(xh, y, 1 - core)
    hdev = smp_dev(1 - xh, y, core)

    def ydev(o, h=0):
        return smp_dev((xh + h) % 2, (y + o) % NY, core)

    others = [(o, h) for o in range(NY) for h in range(2) if o + h > 0]

    sent = []

    class Copy:
        def __init__(self, src, dst, sems, at, dev):
            self.key = (id(sems[1]), at)
            self.copy = pltpu.make_async_remote_copy(
                src_ref=src, dst_ref=dst, send_sem=sems[0].at[at], recv_sem=sems[1].at[at],
                device_id=dev, device_id_type=MESH,
            )

        def start(self):
            self.copy.start()
            sent.append(self)

        def wait_recv(self):
            self.copy.wait_recv()

    def rc(src, dst, sems, at, dev):
        return Copy(src, dst, sems, at, dev)

    barrier = pltpu.get_barrier_semaphore()
    friends = zdev + zdev2 + [xdev, cdev] + [ydev(o, h) for o, h in others]
    for dev in friends:
        pl.semaphore_signal(barrier, inc=1, device_id=dev, device_id_type=MESH)

    loads = [
        pltpu.make_async_copy(src, dst, loc_s.at[n])
        for n, (src, dst) in enumerate(
            ((inter_hbm, ig.at[z, x]), (og_hbm, og), (tw_hbm, tw), (pooled_hbm, pooled), (bags_hbm, bags), (place_hbm, place))
        )
    ]
    for load in loads:
        load.start()
    loads[0].wait()
    pl.semaphore_wait(barrier, len(friends))

    def find_places():
        for l in range(L):
            slot = bags[:, l, :]
            for h in range(2):
                ids = slot[:, h * 128:(h + 1) * 128]
                low, high = ids & 127, ids >> 7
                got = jnp.zeros((F, 128), I32)
                for k in range(4):
                    part = take(place[:, k * 128:(k + 1) * 128], low, 1)
                    got = jnp.where(high == k, part, got)
                got = (got & 0xEF) | (((got >> 8) & 1) << 4) | (((got >> 4) & 1) << 8)
                pl_buf[l * F:(l + 1) * F, h * 128:(h + 1) * 128] = (got - 256).astype(F32)
        iota_buf[...] = (lax.broadcasted_iota(I32, (RT, SB), 0) - 256).astype(F32).astype(BF16)

    RING = ((0, 1), (1, 1), (2, 1), (3, 1))
    RELAY = ((0, 1), (0, 2), (2, 1), (2, 2))

    class Gather:
        def __init__(self, buf, cut, half, hops, za, xa, zb, xb):
            self.buf, self.cut, self.half, self.rows, self.hops = buf, cut, half, buf.shape[2], hops
            self.za, self.xa, self.zb, self.xb = za, xa, zb, xb

        def block(self, d, k, held):
            back = self.hops[k][0] if held else k + 1
            dev = (zdev if self.hops[k][1] == 1 else zdev2)[d]
            return (z + (NZ - back if d == 0 else back)) % NZ, dev

        def first(self, d, k, held):
            zz, dev = self.block(d, k, held)
            lo, hi = (0, self.cut) if k < 3 else ((0, self.half), (self.half, self.cut))[d]
            at = self.buf.at[zz, x, pl.ds(lo, hi - lo)]
            return rc(at, at, self.za, (d, k), dev)

        def across(self, m, xx):
            at = self.buf.at[(z + m) % NZ, xx, pl.ds(0, self.cut)]
            return rc(at, at, self.xa, (m % NZ,), xdev)

        def second(self, i, d, k, held):
            zz, dev = self.block(d, k, held)
            at = self.buf.at[zz, x if i == 0 else 1 - x, pl.ds(self.cut, self.rows - self.cut)]
            return rc(at, at, self.zb, (i, d, k), dev)

        def pair(self, xx):
            at = self.buf.at[z, xx, pl.ds(self.cut, self.rows - self.cut)]
            return rc(at, at, self.xb, (0,), xdev)

        def after(self, k):
            if self.hops is RING:
                return (k,) if k < 4 else ()
            return {0: (0, 1), 2: (2, 3)}.get(k, ())

        def start(self):
            self.pair(x).start()
            for k in self.after(0):
                for d in range(2):
                    self.first(d, k, True).start()
            for k in self.after(0):
                for d in range(2):
                    self.second(0, d, k, True).start()
            self.across(0, x).start()

        def start_pair(self):
            self.pair(1 - x).wait_recv()
            for k in self.after(0):
                for d in range(2):
                    self.second(1, d, k, True).start()

        def hop_first(self, k):
            for d in range(2):
                self.first(d, k - 1, False).wait_recv()
                for n in self.after(k):
                    self.first(d, n, True).start()
                if k < 4:
                    self.across(NZ - k if d == 0 else k, x).start()
            if k == 4:
                self.across(4, x).start()

        def hop_second(self, k):
            for i in range(2):
                for d in range(2):
                    if k < 4 or i == d:
                        self.second(i, d, k - 1, False).wait_recv()
                    for n in self.after(k):
                        if n < 3 or i == d:
                            self.second(i, d, n, True).start()

        def arrived(self, m):
            self.across(m, 1 - x).wait_recv()

    g_inter = Gather(ig, 80, 48, RING, (ia_s, ia_r), (ix_s, ix_r), (ib_s, ib_r), (ip_s, ip_r))
    g_gram = Gather(gg, 48, 32, RELAY, (ga_s, ga_r), (gx_s, gx_r), (gb_s, gb_r), (gp_s, gp_r))
    g_inter.start()
    loads[1].wait()
    loads[2].wait()

    for b in range(6):
        r = lax.dot_general(tw[b * 384:(b + 1) * 384, :], og[...], NT, preferred_element_type=F32)
        for ii in range(8):
            i = b * 8 + ii
            blk = r[ii * F:(ii + 1) * F]
            for row in (i, i + F):
                if row < EXT:
                    for h in range(2):
                        half = blk[:, h * 128:(h + 1) * 128]
                        prod[h, row * EXT:row * EXT + F, :] = half
                        prod[h, row * EXT + F:(row + 1) * EXT, :] = half[:F // 2]
    for d in range(OFF):
        for h in range(2):
            both = prod[h, pl.ds(d, F, stride=EXT + 1), :] + prod[h, pl.ds(EXT * d, F, stride=EXT + 1), :]
            for m in range(3):
                at = d * F + 16 * m
                c, r0 = at // CH, at % CH
                sym[c // NX, c % NX, r0:r0 + 16, h * 128:(h + 1) * 128] = both[16 * m:16 * (m + 1)]
    sym[NZ - 1, NX - 1] = jnp.zeros((CH, SB), F32)

    def dest(d, k):
        return (z + 4 - k) % NZ if d == 0 else (z + 4 + k) % NZ

    def ra_copy(d, k):
        if k == 0:
            return rc(sym.at[dest(d, k), d, pl.ds(0, RA)], ra_buf.at[d, k, d], (ra_s, ra_r), (d, k), zdev[d])
        return rc(sym.at[dest(d, k), :, pl.ds(0, RA)], ra_buf.at[d, k], (ra_s, ra_r), (d, k), zdev[d])

    def ra_step(k):
        for d in range(2):
            if k > 0:
                ra_copy(d, k - 1).wait_recv()
                t = dest(d, k)
                if k == 1:
                    sym[t, d, :RA, :] = sym[t, d, :RA, :] + ra_buf[d, 0, d]
                else:
                    sym[t, :, :RA, :] = sym[t, :, :RA, :] + ra_buf[d, k - 1]
            if k < 4:
                ra_copy(d, k).start()

    def ra_swap():
        return rc(sym.at[z, 1 - x, pl.ds(0, RA)], rx_buf, (rx_s, rx_r), (0,), xdev)

    def bx_copy(m):
        return rc(sym.at[(z + m) % NZ, 1 - x, pl.ds(RA, RB)], bx_buf.at[m], (bx_s, bx_r), (m,), xdev)

    def bx_add(m):
        bx_copy(m).wait_recv()
        t = (z + m) % NZ
        sym[t, x, RA:, :] = sym[t, x, RA:, :] + bx_buf[m]

    def rb_copy(d, k):
        if k == 0:
            part = pl.ds(d * (RB // 2), RB // 2)
            return rc(sym.at[dest(d, k), x, pl.ds(RA + d * (RB // 2), RB // 2)], rb_buf.at[d, k, part], (rb_s, rb_r), (d, k), zdev[d])
        return rc(sym.at[dest(d, k), x, pl.ds(RA, RB)], rb_buf.at[d, k], (rb_s, rb_r), (d, k), zdev[d])

    def rb_step(k):
        if k == 0:
            bx_add(4)
        elif k < 4:
            bx_add(4 - k)
            bx_add(4 + k)
        else:
            bx_add(0)
        for d in range(2):
            if k > 0:
                rb_copy(d, k - 1).wait_recv()
                t = dest(d, k)
                if k == 1:
                    lo = d * (RB // 2)
                    hi = lo + RB // 2
                    sym[t, x, RA + lo:RA + hi, :] = sym[t, x, RA + lo:RA + hi, :] + rb_buf[d, 0, lo:hi, :]
                else:
                    sym[t, x, RA:, :] = sym[t, x, RA:, :] + rb_buf[d, k - 1]
            if k < 4:
                rb_copy(d, k).start()

    def count(f, carry):
        rows = [pl_buf[pl.ds(l * F + f, 1), :].astype(BF16) for l in range(L)]
        for ch in range(4):
            io = iota_buf[ch * 128:(ch + 1) * 128, :]
            acc = jnp.zeros((128, SB), BF16)
            for l in range(L):
                acc = acc + jnp.where(io == rows[l], jnp.ones((), BF16), jnp.zeros((), BF16))
            cnt[f, ch * 128:(ch + 1) * 128, :] = acc
        return carry

    def counts(lo, hi):
        lax.fori_loop(lo, hi, count, 0)

    def w_copy(cb):
        return rc(wt.at[cb, 1 - core], wx.at[cb], (wx_s, wx_r), (cb,), cdev)

    def w_mul(m):
        g_inter.arrived(m)
        zz = (z + m) % NZ
        r = jnp.dot(ig[zz].reshape(2 * IR, SB), og[...], preferred_element_type=F32)
        for q in range(2):
            cb = zz * 2 + q
            for cc in range(2):
                wt[cb, cc] = r[q * IR + cc * WR:q * IR + (cc + 1) * WR]
            w_copy(cb).start()

    def wy_copy(o, h, dev):
        return pltpu.make_async_remote_copy(
            src_ref=ws.at[(y + o) % NY, h], dst_ref=wr.at[o, h], send_sem=wy_s.at[o, h], recv_sem=wy_r.at[o, h],
            device_id=dev, device_id_type=MESH,
        )

    def w_add(m):
        zz = (z + m) % NZ
        for q in range(2):
            cb = zz * 2 + q
            w_copy(cb).wait_recv()
            v = wt[cb, core] + wx[cb]
            h, yy = cb // NY, cb % NY
            ws[yy, h] = jnp.concatenate([v[:, :128], v[:, 128:]], axis=0).astype(BF16)
            o = (yy + NY - y) % NY

            @pl.when(o > 0)
            def _():
                wy_copy(o, h, smp_dev(xh, yy, core)).start()

    ra_step(0)
    for m in (4, 3, 5, 2, 6, 1, 7, 0):
        bx_copy(m).start()
    for n in (3, 4, 5):
        loads[n].wait()
    find_places()
    counts(0, 6)
    g_inter.start_pair()
    counts(6, 14)
    ra_step(1)
    rb_step(0)
    g_inter.hop_first(1)
    g_inter.hop_second(1)
    w_mul(0)
    counts(14, 24)
    ra_step(2)
    rb_step(1)
    g_inter.hop_first(2)
    g_inter.hop_second(2)
    w_add(0)
    w_mul(1)
    w_mul(7)
    counts(24, 32)
    ra_step(3)
    rb_step(2)
    g_inter.hop_first(3)
    g_inter.hop_second(3)
    w_add(1)
    w_add(7)
    w_mul(2)
    w_mul(6)
    counts(32, 40)
    ra_step(4)
    ra_swap().start()
    rb_step(3)
    g_inter.hop_first(4)
    g_inter.hop_second(4)
    w_add(2)
    w_add(6)
    w_mul(3)
    w_mul(5)
    counts(40, F)
    rb_step(4)
    ra_swap().wait_recv()
    gg[z, x, :RA, :] = (sym[z, x, :RA, :] + rx_buf[...]).astype(BF16)
    gg[z, x, RA:, :] = sym[z, x, RA:, :].astype(BF16)
    g_gram.start()
    w_mul(4)
    w_add(3)
    w_add(5)
    g_gram.start_pair()
    w_add(4)
    for j in range(F):
        v = pooled[j].astype(F32)
        pf[j] = v
        pf[j + F] = v
    g_gram.hop_first(1)
    g_gram.hop_first(2)
    g_gram.hop_second(1)
    g_gram.hop_second(2)
    g_gram.hop_first(3)
    g_gram.hop_first(4)
    g_gram.hop_second(3)
    g_gram.hop_second(4)
    for m in range(NZ):
        g_gram.arrived(m)

    for at in range(0, OFF * F, 16):
        c, r0 = at // CH, at % CH
        v = gg[c // NX, c % NX, r0:r0 + 16, :].astype(F32)
        d, i0 = at // F, at % F
        for base in (d * 2 * F + i0, d * 2 * F + F + i0):
            cf[base:base + 16, :] = v

    row = lax.broadcasted_iota(I32, (8, 128), 0)
    lane = lax.broadcasted_iota(I32, (8, 128), 1)
    grp, low4 = lane >> 4, lane & 15
    turn_a = (((grp + row) & 7) << 4) | low4
    turn_b = (row - grp) & 7
    turn_c = (((row - grp) & 7) << 4) | low4

    def pooled_grad(i):
        accs = [jnp.zeros((E8, SB), F32) for _ in range(4)]
        n = 0
        for d in range(OFF):
            accs[n % 4] = accs[n % 4] + cf[pl.ds(i + d * 2 * F, 1), :] * pf[i + d]
            n += 1
        for d in range(1, OFF - 1):
            accs[n % 4] = accs[n % 4] + cf[pl.ds(i + (d * 2 * F + F - d), 1), :] * pf[i + (F - d)]
            n += 1
        v = (accs[0] + accs[1]) + (accs[2] + accs[3])
        hi = v.astype(BF16)
        lo = (v - hi.astype(F32)).astype(BF16)
        return jnp.concatenate([hi, lo], axis=0)

    def table_rows(f, fl, g, halves):
        r = lax.dot_general(halves, cnt[f], NT, preferred_element_type=F32)
        r = r[:E8] + r[E8:]
        for k in range(4):
            v = take(take(take(r[:, k * 128:(k + 1) * 128], turn_a, 1), turn_b, 0), turn_c, 1)
            td[g, k // 2, pl.ds((k % 2) * 128 + fl, 8, stride=GF), :] = v

    def tx_copy(g):
        return rc(td.at[g, 1 - core], tx.at[g], (tx_s, tx_r), (g,), cdev)

    def ty_copy(g, o, h):
        return rc(ts.at[g, (y + o) % NY, (xh + h) % 2], tr.at[g, o, h], (ty_s, ty_r), (g, o, h), ydev(o, h))

    def t_send(g):
        tx_copy(g).wait_recv()
        v = td[g, core] + tx[g]
        ts[g] = v.astype(BF16).reshape(NY, 2, GF, 128)
        for o, h in others:
            ty_copy(g, o, h).start()

    def w_total():
        wtot = ws[y].astype(F32)
        for o in range(1, NY):
            for h in range(2):
                wy_copy(o, h, ydev(o)).wait_recv()
            wtot = wtot + wr[o].astype(F32)
        wf[...] = wtot
        ws[y] = wtot.astype(BF16)
        whc = rc(ws.at[y, 1 - xh], wxh, (wh_s, wh_r), (0,), hdev)
        whc.start()
        return whc

    halves = pooled_grad(0)
    for g in range(NG):
        def body(fl, halves, g=g):
            table_rows(g * GF + fl, fl, g, halves)
            return pooled_grad(g * GF + fl + 1)

        halves = lax.fori_loop(0, GF, body, halves, unroll=GF)
        tx_copy(g).start()
        if g == 0:
            whc = w_total()
        if g > 0:
            t_send(g - 1)
    t_send(NG - 1)

    for g in range(NG):
        tot = ts[g, y, xh].astype(F32)
        for o, h in others:
            ty_copy(g, o, h).wait_recv()
            tot = tot + tr[g, o, h].astype(F32)
        t_out[g * GF:(g + 1) * GF, :] = tot
    whc.wait_recv()
    tot = wf[xh] + wxh[...].astype(F32)
    w_out[...] = tot

    for o in range(1, NY):
        for h in range(2):
            wy_copy(o, h, ydev(o)).wait_send()
    for copy in sent:
        copy.copy.wait_send()


def finish(w_sum, t_sum, w_out, t_out):
    w_out[:, :128] = w_sum[:WR]
    w_out[:, 128:] = w_sum[WR:]
    t_out[...] = t_sum[...].T.reshape(E8, 16, F)


def shards(interaction, out_grad, top_weight, pooled, bags, row_place):
    dma = pltpu.SemaphoreType.DMA
    v = pltpu.VMEM
    vmem = pl.BlockSpec(memory_space=pltpu.VMEM)
    gather_sems = [dma(n) for n in ((2, 4), (NZ,), (2, 2, 4), (1,)) for _ in range(2)]
    outs = pl.pallas_call(
        kernel,
        out_shape=(
            jax.ShapeDtypeStruct((2 * WR, 128), F32),
            jax.ShapeDtypeStruct((F, 128), F32),
        ),
        in_specs=[pl.BlockSpec(memory_space=pl.ANY)] * 6,
        out_specs=(vmem, vmem),
        scratch_shapes=[
            v((SB, HB), BF16), v((F * F, HB), BF16), v((F, E8, SB), BF16), v((F, L, SB), I32), v((F, RT), I32),
            v((2, EXT * EXT, 128), F32),
            v((NZ, NX, CH, SB), F32),
            v((2, 4, NX, RA, SB), F32),
            v((2, 4, RB, SB), F32),
            v((NZ, RB, SB), F32),
            v((RA, SB), F32),
            v((NZ, NX, CH, SB), BF16),
            v((OFF * 2 * F, SB), F32),
            v((2 * F, E8, SB), F32),
            v((L * F, SB), F32),
            v((RT, SB), BF16),
            v((F, RT, SB), BF16),
            v((NZ, NX, IR, SB), BF16),
            v((16, 2, WR, HB), F32),
            v((16, WR, HB), F32),
            v((NY, 2, 2 * WR, 128), BF16),
            v((NY, 2, 2 * WR, 128), BF16),
            v((2, 2 * WR, 128), F32),
            v((2 * WR, 128), BF16),
            v((NG, 2, 16 * GF, 128), F32),
            v((NG, 16 * GF, 128), F32),
            v((NG, NY, 2, GF, 128), BF16),
            v((NG, NY, 2, GF, 128), BF16),
            dma((2, 4)), dma((2, 4)), dma((2, 4)), dma((2, 4)), dma((NZ,)), dma((NZ,)), dma((1,)), dma((1,)),
            *gather_sems, *gather_sems,
            dma((16,)), dma((16,)), dma((NY, 2)), dma((NY, 2)), dma((1,)), dma((1,)),
            dma((NG,)), dma((NG,)), dma((NG, NY, 2)), dma((NG, NY, 2)),
            dma((6,)),
        ],
        compiler_params=pltpu.CompilerParams(
            collective_id=0, has_side_effects=True, vmem_limit_bytes=56 * 1024 * 1024
        ),
    )(interaction, out_grad, top_weight, pooled, bags, row_place)
    weights, tables = pl.pallas_call(
        finish,
        out_shape=(
            jax.ShapeDtypeStruct((WR, HB), F32),
            jax.ShapeDtypeStruct((E8, 16, F), F32),
        ),
        in_specs=[vmem, vmem],
        out_specs=(vmem, vmem),
    )(*outs)
    return weights, jnp.transpose(tables, (0, 2, 1))


def solution(mesh):
    in_specs = (
        P("col", "sample"),
        P("sample", "col"),
        P(None, "col"),
        P(None, "col", "sample"),
        P(None, None, "sample"),
        P(),
    )
    out_specs = (P("sample", "col"), P("col", None, "sample"))
    return jax.shard_map(shards, mesh=mesh, in_specs=in_specs, out_specs=out_specs, check_vma=False)
```

```python
import jax
import jax.numpy as jnp
from jax import lax
from jax.experimental import pallas as pl
from jax.experimental.pallas import tpu as pltpu
from jax.sharding import PartitionSpec as P

MESH = pl.DeviceIdType.MESH
F32, BF16, I32 = jnp.float32, jnp.bfloat16, jnp.int32

F, E8, SB, HB, L, RT = 48, 8, 256, 256, 4, 512
NZ, NX, NY = 8, 2, 8
OFF = F // 2 + 1
CH = 80
RA, RB = 32, 48
WR = 72
IR = 144
GF = 16
NG = F // GF
EXT = F + F // 2
NT = (((1,), (1,)), ((), ()))


def take(v, at, axis):
    return jnp.take_along_axis(v, at, axis=axis, mode="promise_in_bounds")


def kernel(
    inter_hbm, og_hbm, tw_hbm, pooled_hbm, bags_hbm, place_hbm,
    w_out, t_out,
    og, tw, pooled, bags, place,
    prod, sym, ra_buf, rb_buf, bx_buf, rx_buf, gg, cf, pf, pl_buf, iota_buf, cnt,
    ig, wt, wx, ws, wr, wf, wxh,
    td, tx, ts, tr,
    ra_s, ra_r, rb_s, rb_r, bx_s, bx_r, rx_s, rx_r,
    ga_s, ga_r, gx_s, gx_r, gb_s, gb_r, gp_s, gp_r,
    ia_s, ia_r, ix_s, ix_r, ib_s, ib_r, ip_s, ip_r,
    wx_s, wx_r, wy_s, wy_r, wh_s, wh_r, tx_s, tx_r, ty_s, ty_r,
    loc_s,
):
    col, smp = lax.axis_index("col"), lax.axis_index("sample")
    z, x = col // NX, col % NX
    xh, y, core = smp // 16, (smp // 2) % NY, smp % 2

    def col_dev(zz, xx):
        return {"col": zz * NX + xx, "sample": smp}

    def smp_dev(hh, yy, cc):
        return {"col": col, "sample": hh * 16 + yy * 2 + cc}

    zdev = [col_dev((z + 1) % NZ, x), col_dev((z + NZ - 1) % NZ, x)]
    zdev2 = [col_dev((z + 2) % NZ, x), col_dev((z + NZ - 2) % NZ, x)]
    xdev = col_dev(z, 1 - x)
    cdev = smp_dev(xh, y, 1 - core)
    hdev = smp_dev(1 - xh, y, core)

    def ydev(o, h=0):
        return smp_dev((xh + h) % 2, (y + o) % NY, core)

    others = [(o, h) for o in range(NY) for h in range(2) if o + h > 0]

    sent = []

    class Copy:
        def __init__(self, src, dst, sems, at, dev):
            self.key = (id(sems[1]), at)
            self.copy = pltpu.make_async_remote_copy(
                src_ref=src, dst_ref=dst, send_sem=sems[0].at[at], recv_sem=sems[1].at[at],
                device_id=dev, device_id_type=MESH,
            )

        def start(self):
            self.copy.start()
            sent.append(self)

        def wait_recv(self):
            self.copy.wait_recv()

    def rc(src, dst, sems, at, dev):
        return Copy(src, dst, sems, at, dev)

    barrier = pltpu.get_barrier_semaphore()
    friends = zdev + zdev2 + [xdev, cdev] + [ydev(o, h) for o, h in others]
    for dev in friends:
        pl.semaphore_signal(barrier, inc=1, device_id=dev, device_id_type=MESH)

    loads = [
        pltpu.make_async_copy(src, dst, loc_s.at[n])
        for n, (src, dst) in enumerate(
            ((inter_hbm, ig.at[z, x]), (og_hbm, og), (tw_hbm, tw), (pooled_hbm, pooled), (bags_hbm, bags), (place_hbm, place))
        )
    ]
    for load in loads:
        load.start()
    loads[0].wait()
    pl.semaphore_wait(barrier, len(friends))

    def find_places():
        for l in range(L):
            slot = bags[:, l, :]
            for h in range(2):
                ids = slot[:, h * 128:(h + 1) * 128]
                low, high = ids & 127, ids >> 7
                got = jnp.zeros((F, 128), I32)
                for k in range(4):
                    part = take(place[:, k * 128:(k + 1) * 128], low, 1)
                    got = jnp.where(high == k, part, got)
                got = (got & 0xEF) | (((got >> 8) & 1) << 4) | (((got >> 4) & 1) << 8)
                pl_buf[l * F:(l + 1) * F, h * 128:(h + 1) * 128] = (got - 256).astype(F32)
        iota_buf[...] = (lax.broadcasted_iota(I32, (RT, SB), 0) - 256).astype(F32).astype(BF16)

    RING = ((0, 1), (1, 1), (2, 1), (3, 1))
    RELAY = ((0, 1), (0, 2), (2, 1), (2, 2))

    class Gather:
        def __init__(self, buf, cut, half, hops, za, xa, zb, xb):
            self.buf, self.cut, self.half, self.rows, self.hops = buf, cut, half, buf.shape[2], hops
            self.za, self.xa, self.zb, self.xb = za, xa, zb, xb

        def block(self, d, k, held):
            back = self.hops[k][0] if held else k + 1
            dev = (zdev if self.hops[k][1] == 1 else zdev2)[d]
            return (z + (NZ - back if d == 0 else back)) % NZ, dev

        def first(self, d, k, held):
            zz, dev = self.block(d, k, held)
            lo, hi = (0, self.cut) if k < 3 else ((0, self.half), (self.half, self.cut))[d]
            at = self.buf.at[zz, x, pl.ds(lo, hi - lo)]
            return rc(at, at, self.za, (d, k), dev)

        def across(self, m, xx):
            at = self.buf.at[(z + m) % NZ, xx, pl.ds(0, self.cut)]
            return rc(at, at, self.xa, (m % NZ,), xdev)

        def second(self, i, d, k, held):
            zz, dev = self.block(d, k, held)
            at = self.buf.at[zz, x if i == 0 else 1 - x, pl.ds(self.cut, self.rows - self.cut)]
            return rc(at, at, self.zb, (i, d, k), dev)

        def pair(self, xx):
            at = self.buf.at[z, xx, pl.ds(self.cut, self.rows - self.cut)]
            return rc(at, at, self.xb, (0,), xdev)

        def after(self, k):
            if self.hops is RING:
                return (k,) if k < 4 else ()
            return {0: (0, 1), 2: (2, 3)}.get(k, ())

        def start(self):
            self.pair(x).start()
            for k in self.after(0):
                for d in range(2):
                    self.first(d, k, True).start()
            for k in self.after(0):
                for d in range(2):
                    self.second(0, d, k, True).start()

        def start_pair(self):
            self.pair(1 - x).wait_recv()
            for k in self.after(0):
                for d in range(2):
                    self.second(1, d, k, True).start()

        def hop_first(self, k):
            for d in range(2):
                self.first(d, k - 1, False).wait_recv()
                for n in self.after(k):
                    self.first(d, n, True).start()
                if k < 4:
                    self.across(NZ - k if d == 0 else k, x).start()
            if k == 4:
                self.across(4, x).start()

        def hop_second(self, k):
            for i in range(2):
                for d in range(2):
                    if k < 4 or i == d:
                        self.second(i, d, k - 1, False).wait_recv()
                    for n in self.after(k):
                        if n < 3 or i == d:
                            self.second(i, d, n, True).start()

        def arrived(self, m):
            self.across(m, 1 - x).wait_recv()

    g_inter = Gather(ig, 80, 48, RING, (ia_s, ia_r), (ix_s, ix_r), (ib_s, ib_r), (ip_s, ip_r))
    g_gram = Gather(gg, 48, 32, RELAY, (ga_s, ga_r), (gx_s, gx_r), (gb_s, gb_r), (gp_s, gp_r))
    g_inter.start()
    loads[1].wait()
    loads[2].wait()

    for b in range(6):
        r = lax.dot_general(tw[b * 384:(b + 1) * 384, :], og[...], NT, preferred_element_type=F32)
        for ii in range(8):
            i = b * 8 + ii
            blk = r[ii * F:(ii + 1) * F]
            for row in (i, i + F):
                if row < EXT:
                    for h in range(2):
                        half = blk[:, h * 128:(h + 1) * 128]
                        prod[h, row * EXT:row * EXT + F, :] = half
                        prod[h, row * EXT + F:(row + 1) * EXT, :] = half[:F // 2]
    for d in range(OFF):
        for h in range(2):
            both = prod[h, pl.ds(d, F, stride=EXT + 1), :] + prod[h, pl.ds(EXT * d, F, stride=EXT + 1), :]
            for m in range(3):
                at = d * F + 16 * m
                c, r0 = at // CH, at % CH
                sym[c // NX, c % NX, r0:r0 + 16, h * 128:(h + 1) * 128] = both[16 * m:16 * (m + 1)]
    sym[NZ - 1, NX - 1] = jnp.zeros((CH, SB), F32)

    def dest(d, k):
        return (z + 4 - k) % NZ if d == 0 else (z + 4 + k) % NZ

    def ra_copy(d, k):
        if k == 0:
            return rc(sym.at[dest(d, k), d, pl.ds(0, RA)], ra_buf.at[d, k, d], (ra_s, ra_r), (d, k), zdev[d])
        return rc(sym.at[dest(d, k), :, pl.ds(0, RA)], ra_buf.at[d, k], (ra_s, ra_r), (d, k), zdev[d])

    def ra_step(k):
        for d in range(2):
            if k > 0:
                ra_copy(d, k - 1).wait_recv()
                t = dest(d, k)
                if k == 1:
                    sym[t, d, :RA, :] = sym[t, d, :RA, :] + ra_buf[d, 0, d]
                else:
                    sym[t, :, :RA, :] = sym[t, :, :RA, :] + ra_buf[d, k - 1]
            if k < 4:
                ra_copy(d, k).start()

    def ra_swap():
        return rc(sym.at[z, 1 - x, pl.ds(0, RA)], rx_buf, (rx_s, rx_r), (0,), xdev)

    def bx_copy(m):
        return rc(sym.at[(z + m) % NZ, 1 - x, pl.ds(RA, RB)], bx_buf.at[m], (bx_s, bx_r), (m,), xdev)

    def bx_add(m):
        bx_copy(m).wait_recv()
        t = (z + m) % NZ
        sym[t, x, RA:, :] = sym[t, x, RA:, :] + bx_buf[m]

    def rb_copy(d, k):
        if k == 0:
            part = pl.ds(d * (RB // 2), RB // 2)
            return rc(sym.at[dest(d, k), x, pl.ds(RA + d * (RB // 2), RB // 2)], rb_buf.at[d, k, part], (rb_s, rb_r), (d, k), zdev[d])
        return rc(sym.at[dest(d, k), x, pl.ds(RA, RB)], rb_buf.at[d, k], (rb_s, rb_r), (d, k), zdev[d])

    def rb_step(k):
        if k == 0:
            bx_add(4)
        elif k < 4:
            bx_add(4 - k)
            bx_add(4 + k)
        else:
            bx_add(0)
        for d in range(2):
            if k > 0:
                rb_copy(d, k - 1).wait_recv()
                t = dest(d, k)
                if k == 1:
                    lo = d * (RB // 2)
                    hi = lo + RB // 2
                    sym[t, x, RA + lo:RA + hi, :] = sym[t, x, RA + lo:RA + hi, :] + rb_buf[d, 0, lo:hi, :]
                else:
                    sym[t, x, RA:, :] = sym[t, x, RA:, :] + rb_buf[d, k - 1]
            if k < 4:
                rb_copy(d, k).start()

    def count(f, carry):
        rows = [pl_buf[pl.ds(l * F + f, 1), :].astype(BF16) for l in range(L)]
        for ch in range(4):
            io = iota_buf[ch * 128:(ch + 1) * 128, :]
            acc = jnp.zeros((128, SB), BF16)
            for l in range(L):
                acc = acc + jnp.where(io == rows[l], jnp.ones((), BF16), jnp.zeros((), BF16))
            cnt[f, ch * 128:(ch + 1) * 128, :] = acc
        return carry

    def counts(lo, hi):
        lax.fori_loop(lo, hi, count, 0)

    def w_copy(cb):
        return rc(wt.at[cb, 1 - core], wx.at[cb], (wx_s, wx_r), (cb,), cdev)

    def w_mul(m):
        g_inter.arrived(m)
        zz = (z + m) % NZ
        r = jnp.dot(ig[zz].reshape(2 * IR, SB), og[...], preferred_element_type=F32)
        for q in range(2):
            cb = zz * 2 + q
            for cc in range(2):
                wt[cb, cc] = r[q * IR + cc * WR:q * IR + (cc + 1) * WR]
            w_copy(cb).start()

    def wy_copy(o, h, dev):
        return pltpu.make_async_remote_copy(
            src_ref=ws.at[(y + o) % NY, h], dst_ref=wr.at[o, h], send_sem=wy_s.at[o, h], recv_sem=wy_r.at[o, h],
            device_id=dev, device_id_type=MESH,
        )

    def w_add(m):
        zz = (z + m) % NZ
        for q in range(2):
            cb = zz * 2 + q
            w_copy(cb).wait_recv()
            v = wt[cb, core] + wx[cb]
            h, yy = cb // NY, cb % NY
            ws[yy, h] = jnp.concatenate([v[:, :128], v[:, 128:]], axis=0).astype(BF16)
            o = (yy + NY - y) % NY

            @pl.when(o > 0)
            def _():
                wy_copy(o, h, smp_dev(xh, yy, core)).start()

    ra_step(0)
    for m in (4, 3, 5):
        bx_copy(m).start()
    g_inter.across(0, x).start()
    for n in (3, 4, 5):
        loads[n].wait()
    find_places()
    counts(0, 6)
    g_inter.start_pair()
    counts(6, 14)
    ra_step(1)
    rb_step(0)
    bx_copy(2).start()
    bx_copy(6).start()
    g_inter.hop_first(1)
    g_inter.hop_second(1)
    w_mul(0)
    counts(14, 24)
    ra_step(2)
    rb_step(1)
    bx_copy(1).start()
    bx_copy(7).start()
    g_inter.hop_first(2)
    g_inter.hop_second(2)
    w_add(0)
    w_mul(1)
    w_mul(7)
    counts(24, 32)
    ra_step(3)
    rb_step(2)
    bx_copy(0).start()
    g_inter.hop_first(3)
    g_inter.hop_second(3)
    w_add(1)
    w_add(7)
    w_mul(2)
    w_mul(6)
    counts(32, 40)
    ra_step(4)
    ra_swap().start()
    rb_step(3)
    g_inter.hop_first(4)
    g_inter.hop_second(4)
    w_add(2)
    w_add(6)
    w_mul(3)
    w_mul(5)
    counts(40, F)
    rb_step(4)
    ra_swap().wait_recv()
    gg[z, x, :RA, :] = (sym[z, x, :RA, :] + rx_buf[...]).astype(BF16)
    gg[z, x, RA:, :] = sym[z, x, RA:, :].astype(BF16)
    g_gram.start()
    g_gram.across(0, x).start()
    w_mul(4)
    w_add(3)
    w_add(5)
    g_gram.start_pair()
    w_add(4)
    for j in range(F):
        v = pooled[j].astype(F32)
        pf[j] = v
        pf[j + F] = v
    g_gram.hop_first(1)
    g_gram.hop_first(2)
    g_gram.hop_second(1)
    g_gram.hop_second(2)
    g_gram.hop_first(3)
    g_gram.hop_first(4)
    g_gram.hop_second(3)
    g_gram.hop_second(4)
    for m in range(NZ):
        g_gram.arrived(m)

    for at in range(0, OFF * F, 16):
        c, r0 = at // CH, at % CH
        v = gg[c // NX, c % NX, r0:r0 + 16, :].astype(F32)
        d, i0 = at // F, at % F
        for base in (d * 2 * F + i0, d * 2 * F + F + i0):
            cf[base:base + 16, :] = v

    row = lax.broadcasted_iota(I32, (8, 128), 0)
    lane = lax.broadcasted_iota(I32, (8, 128), 1)
    grp, low4 = lane >> 4, lane & 15
    turn_a = (((grp + row) & 7) << 4) | low4
    turn_b = (row - grp) & 7
    turn_c = (((row - grp) & 7) << 4) | low4

    def pooled_grad(i):
        accs = [jnp.zeros((E8, SB), F32) for _ in range(4)]
        n = 0
        for d in range(OFF):
            accs[n % 4] = accs[n % 4] + cf[pl.ds(i + d * 2 * F, 1), :] * pf[i + d]
            n += 1
        for d in range(1, OFF - 1):
            accs[n % 4] = accs[n % 4] + cf[pl.ds(i + (d * 2 * F + F - d), 1), :] * pf[i + (F - d)]
            n += 1
        v = (accs[0] + accs[1]) + (accs[2] + accs[3])
        hi = v.astype(BF16)
        lo = (v - hi.astype(F32)).astype(BF16)
        return jnp.concatenate([hi, lo], axis=0)

    def table_rows(f, fl, g, halves):
        r = lax.dot_general(halves, cnt[f], NT, preferred_element_type=F32)
        r = r[:E8] + r[E8:]
        for k in range(4):
            v = take(take(take(r[:, k * 128:(k + 1) * 128], turn_a, 1), turn_b, 0), turn_c, 1)
            td[g, k // 2, pl.ds((k % 2) * 128 + fl, 8, stride=GF), :] = v

    def tx_copy(g):
        return rc(td.at[g, 1 - core, pl.ds(0, 16 * GF)], tx.at[g], (tx_s, tx_r), (g,), cdev)

    def ty_copy(g, o, h):
        return rc(ts.at[g, (y + o) % NY, (xh + h) % 2], tr.at[g, o, h], (ty_s, ty_r), (g, o, h), ydev(o, h))

    def t_send(g):
        tx_copy(g).wait_recv()
        v = td[g, core, :16 * GF, :] + tx[g]
        ts[g] = v.astype(BF16).reshape(NY, 2, GF, 128)
        for o, h in others:
            ty_copy(g, o, h).start()

    def w_total():
        wtot = ws[y].astype(F32)
        for o in range(1, NY):
            for h in range(2):
                wy_copy(o, h, ydev(o)).wait_recv()
            wtot = wtot + wr[o].astype(F32)
        wf[...] = wtot
        ws[y] = wtot.astype(BF16)
        whc = rc(ws.at[y, 1 - xh], wxh, (wh_s, wh_r), (0,), hdev)
        whc.start()
        return whc

    halves = pooled_grad(0)
    for g in range(NG):
        def body(fl, halves, g=g):
            table_rows(g * GF + fl, fl, g, halves)
            return pooled_grad(g * GF + fl + 1)

        halves = lax.fori_loop(0, GF, body, halves, unroll=GF)
        tx_copy(g).start()
        if g > 0:
            t_send(g - 1)
    whc = w_total()
    t_send(NG - 1)

    for g in range(NG):
        tot = ts[g, y, xh].astype(F32)
        for o, h in others:
            ty_copy(g, o, h).wait_recv()
            tot = tot + tr[g, o, h].astype(F32)
        t_out[g * GF:(g + 1) * GF, :] = tot
    whc.wait_recv()
    tot = wf[xh] + wxh[...].astype(F32)
    w_out[...] = tot

    for o in range(1, NY):
        for h in range(2):
            wy_copy(o, h, ydev(o)).wait_send()
    for copy in sent:
        copy.copy.wait_send()


def finish(w_sum, t_sum, w_out, t_out):
    w_out[:, :128] = w_sum[:WR]
    w_out[:, 128:] = w_sum[WR:]
    t_out[...] = t_sum[...].T.reshape(E8, 16, F)


def shards(interaction, out_grad, top_weight, pooled, bags, row_place):
    dma = pltpu.SemaphoreType.DMA
    v = pltpu.VMEM
    vmem = pl.BlockSpec(memory_space=pltpu.VMEM)
    gather_sems = [dma(n) for n in ((2, 4), (NZ,), (2, 2, 4), (1,)) for _ in range(2)]
    outs = pl.pallas_call(
        kernel,
        out_shape=(
            jax.ShapeDtypeStruct((2 * WR, 128), F32),
            jax.ShapeDtypeStruct((F, 128), F32),
        ),
        in_specs=[pl.BlockSpec(memory_space=pl.ANY)] * 6,
        out_specs=(vmem, vmem),
        scratch_shapes=[
            v((SB, HB), BF16), v((F * F, HB), BF16), v((F, E8, SB), BF16), v((F, L, SB), I32), v((F, RT), I32),
            v((2, EXT * (EXT + 2), 128), F32),
            v((NZ, NX, CH, SB), F32),
            v((2, 4, NX, RA, SB), F32),
            v((2, 4, RB, SB), F32),
            v((NZ, RB, SB), F32),
            v((RA, SB), F32),
            v((NZ, NX, CH, SB), BF16),
            v((OFF * 2 * F, SB), F32),
            v((2 * F, E8, SB), F32),
            v((L * F, SB), F32),
            v((RT, SB), BF16),
            v((F, RT, SB), BF16),
            v((NZ, NX, IR, SB), BF16),
            v((16, 2, WR, HB), F32),
            v((16, WR, HB), F32),
            v((NY, 2, 2 * WR, 128), BF16),
            v((NY, 2, 2 * WR, 128), BF16),
            v((2, 2 * WR, 128), F32),
            v((2 * WR, 128), BF16),
            v((NG, 2, 17 * GF, 128), F32),
            v((NG, 16 * GF, 128), F32),
            v((NG, NY, 2, GF, 128), BF16),
            v((NG, NY, 2, GF, 128), BF16),
            dma((2, 4)), dma((2, 4)), dma((2, 4)), dma((2, 4)), dma((NZ,)), dma((NZ,)), dma((1,)), dma((1,)),
            *gather_sems, *gather_sems,
            dma((16,)), dma((16,)), dma((NY, 2)), dma((NY, 2)), dma((1,)), dma((1,)),
            dma((NG,)), dma((NG,)), dma((NG, NY, 2)), dma((NG, NY, 2)),
            dma((6,)),
        ],
        compiler_params=pltpu.CompilerParams(
            collective_id=0, has_side_effects=True, vmem_limit_bytes=56 * 1024 * 1024
        ),
    )(interaction, out_grad, top_weight, pooled, bags, row_place)
    weights, tables = pl.pallas_call(
        finish,
        out_shape=(
            jax.ShapeDtypeStruct((WR, HB), F32),
            jax.ShapeDtypeStruct((E8, 16, F), F32),
        ),
        in_specs=[vmem, vmem],
        out_specs=(vmem, vmem),
    )(*outs)
    return weights, jnp.transpose(tables, (0, 2, 1))


def solution(mesh):
    in_specs = (
        P("col", "sample"),
        P("sample", "col"),
        P(None, "col"),
        P(None, "col", "sample"),
        P(None, None, "sample"),
        P(),
    )
    out_specs = (P("sample", "col"), P("col", None, "sample"))
    return jax.shard_map(shards, mesh=mesh, in_specs=in_specs, out_specs=out_specs, check_vma=False)
```

```python
import jax
import jax.numpy as jnp
from jax import lax
from jax.experimental import pallas as pl
from jax.experimental.pallas import tpu as pltpu
from jax.sharding import PartitionSpec as P

MESH = pl.DeviceIdType.MESH
F32, BF16, I32 = jnp.float32, jnp.bfloat16, jnp.int32

F, E8, SB, HB, L, RT = 48, 8, 256, 256, 4, 512
NZ, NX, NY = 8, 2, 8
OFF = F // 2 + 1
CH = 80
RA, RB = 32, 48
WR = 72
IR = 144
GF = 16
NG = F // GF
EXT = F + F // 2
NT = (((1,), (1,)), ((), ()))


def take(v, at, axis):
    return jnp.take_along_axis(v, at, axis=axis, mode="promise_in_bounds")


def kernel(
    inter_hbm, og_hbm, tw_hbm, pooled_hbm, bags_hbm, place_hbm,
    w_out, t_out,
    og, tw, pooled, bags, place,
    prod, sym, ra_buf, rb_buf, bx_buf, rx_buf, gg, cf, pf, pl_buf, iota_buf, cnt,
    ig, wt, wx, ws, wr, wf, wxh,
    td, tx, ts, tr,
    ra_s, ra_r, rb_s, rb_r, bx_s, bx_r, rx_s, rx_r,
    ga_s, ga_r, gx_s, gx_r, gb_s, gb_r, gp_s, gp_r,
    ia_s, ia_r, ix_s, ix_r, ib_s, ib_r, ip_s, ip_r,
    wx_s, wx_r, wy_s, wy_r, wh_s, wh_r, tx_s, tx_r, ty_s, ty_r,
    loc_s,
):
    col, smp = lax.axis_index("col"), lax.axis_index("sample")
    z, x = col // NX, col % NX
    xh, y, core = smp // 16, (smp // 2) % NY, smp % 2

    def col_dev(zz, xx):
        return {"col": zz * NX + xx, "sample": smp}

    def smp_dev(hh, yy, cc):
        return {"col": col, "sample": hh * 16 + yy * 2 + cc}

    zdev = [col_dev((z + 1) % NZ, x), col_dev((z + NZ - 1) % NZ, x)]
    zdev2 = [col_dev((z + 2) % NZ, x), col_dev((z + NZ - 2) % NZ, x)]
    xdev = col_dev(z, 1 - x)
    cdev = smp_dev(xh, y, 1 - core)
    hdev = smp_dev(1 - xh, y, core)

    def ydev(o, h=0):
        return smp_dev((xh + h) % 2, (y + o) % NY, core)

    others = [(o, h) for o in range(NY) for h in range(2) if o + h > 0]

    sent = []

    class Copy:
        def __init__(self, src, dst, sems, at, dev):
            self.key = (id(sems[1]), at)
            self.copy = pltpu.make_async_remote_copy(
                src_ref=src, dst_ref=dst, send_sem=sems[0].at[at], recv_sem=sems[1].at[at],
                device_id=dev, device_id_type=MESH,
            )

        def start(self):
            self.copy.start()
            sent.append(self)

        def wait_recv(self):
            self.copy.wait_recv()

    def rc(src, dst, sems, at, dev):
        return Copy(src, dst, sems, at, dev)

    barrier = pltpu.get_barrier_semaphore()
    friends = zdev + zdev2 + [xdev, cdev] + [ydev(o, h) for o, h in others]
    for dev in reversed(friends):
        pl.semaphore_signal(barrier, inc=1, device_id=dev, device_id_type=MESH)

    loads = [
        pltpu.make_async_copy(src, dst, loc_s.at[n])
        for n, (src, dst) in enumerate(
            ((inter_hbm, ig.at[z, x]), (og_hbm, og), (tw_hbm, tw), (pooled_hbm, pooled), (bags_hbm, bags), (place_hbm, place))
        )
    ]
    for load in loads:
        load.start()
    loads[0].wait()
    pl.semaphore_wait(barrier, len(friends))

    def find_places():
        for l in range(L):
            slot = bags[:, l, :]
            for h in range(2):
                ids = slot[:, h * 128:(h + 1) * 128]
                low, high = ids & 127, ids >> 7
                got = jnp.zeros((F, 128), I32)
                for k in range(4):
                    part = take(place[:, k * 128:(k + 1) * 128], low, 1)
                    got = jnp.where(high == k, part, got)
                got = (got & 0xEF) | (((got >> 8) & 1) << 4) | (((got >> 4) & 1) << 8)
                pl_buf[l * F:(l + 1) * F, h * 128:(h + 1) * 128] = (got - 256).astype(F32)
        iota_buf[...] = (lax.broadcasted_iota(I32, (RT, SB), 0) - 256).astype(F32).astype(BF16)

    RING = ((0, 1), (1, 1), (2, 1), (3, 1))
    RELAY = ((0, 1), (0, 2), (2, 1), (2, 2))

    class Gather:
        def __init__(self, buf, cut, half, hops, za, xa, zb, xb):
            self.buf, self.cut, self.half, self.rows, self.hops = buf, cut, half, buf.shape[2], hops
            self.za, self.xa, self.zb, self.xb = za, xa, zb, xb

        def block(self, d, k, held):
            back = self.hops[k][0] if held else k + 1
            dev = (zdev if self.hops[k][1] == 1 else zdev2)[d]
            return (z + (NZ - back if d == 0 else back)) % NZ, dev

        def first(self, d, k, held):
            zz, dev = self.block(d, k, held)
            lo, hi = (0, self.cut) if k < 3 else ((0, self.half), (self.half, self.cut))[d]
            at = self.buf.at[zz, x, pl.ds(lo, hi - lo)]
            return rc(at, at, self.za, (d, k), dev)

        def across(self, m, xx):
            at = self.buf.at[(z + m) % NZ, xx, pl.ds(0, self.cut)]
            return rc(at, at, self.xa, (m % NZ,), xdev)

        def second(self, i, d, k, held):
            zz, dev = self.block(d, k, held)
            at = self.buf.at[zz, x if i == 0 else 1 - x, pl.ds(self.cut, self.rows - self.cut)]
            return rc(at, at, self.zb, (i, d, k), dev)

        def pair(self, xx):
            at = self.buf.at[z, xx, pl.ds(self.cut, self.rows - self.cut)]
            return rc(at, at, self.xb, (0,), xdev)

        def after(self, k):
            if self.hops is RING:
                return (k,) if k < 4 else ()
            return {0: (0, 1), 2: (2, 3)}.get(k, ())

        def start(self):
            self.pair(x).start()
            for k in self.after(0):
                for d in range(2):
                    self.first(d, k, True).start()
            for k in self.after(0):
                for d in range(2):
                    self.second(0, d, k, True).start()

        def start_pair(self):
            self.pair(1 - x).wait_recv()
            for k in self.after(0):
                for d in range(2):
                    self.second(1, d, k, True).start()

        def hop_first(self, k):
            for d in range(2):
                self.first(d, k - 1, False).wait_recv()
                for n in self.after(k):
                    self.first(d, n, True).start()
                if k < 4:
                    self.across(NZ - k if d == 0 else k, x).start()
            if k == 4:
                self.across(4, x).start()

        def hop_second(self, k):
            for i in range(2):
                for d in range(2):
                    if k < 4 or i == d:
                        self.second(i, d, k - 1, False).wait_recv()
                    for n in self.after(k):
                        if n < 3 or i == d:
                            self.second(i, d, n, True).start()

        def arrived(self, m):
            self.across(m, 1 - x).wait_recv()

    g_inter = Gather(ig, 80, 48, RING, (ia_s, ia_r), (ix_s, ix_r), (ib_s, ib_r), (ip_s, ip_r))
    g_gram = Gather(gg, 48, 32, RELAY, (ga_s, ga_r), (gx_s, gx_r), (gb_s, gb_r), (gp_s, gp_r))
    g_inter.start()
    loads[1].wait()
    loads[2].wait()

    for b in range(6):
        r = lax.dot_general(tw[b * 384:(b + 1) * 384, :], og[...], NT, preferred_element_type=F32)
        for ii in range(8):
            i = b * 8 + ii
            blk = r[ii * F:(ii + 1) * F]
            for row in (i, i + F):
                if row < EXT:
                    for h in range(2):
                        half = blk[:, h * 128:(h + 1) * 128]
                        prod[h, row * EXT:row * EXT + F, :] = half
                        prod[h, row * EXT + F:(row + 1) * EXT, :] = half[:F // 2]
    for d in range(OFF):
        for h in range(2):
            both = prod[h, pl.ds(d, F, stride=EXT + 1), :] + prod[h, pl.ds(EXT * d, F, stride=EXT + 1), :]
            for m in range(3):
                at = d * F + 16 * m
                c, r0 = at // CH, at % CH
                sym[c // NX, c % NX, r0:r0 + 16, h * 128:(h + 1) * 128] = both[16 * m:16 * (m + 1)]
    sym[NZ - 1, NX - 1] = jnp.zeros((CH, SB), F32)

    def dest(d, k):
        return (z + 4 - k) % NZ if d == 0 else (z + 4 + k) % NZ

    def ra_copy(d, k):
        if k == 0:
            return rc(sym.at[dest(d, k), d, pl.ds(0, RA)], ra_buf.at[d, k, d], (ra_s, ra_r), (d, k), zdev[d])
        return rc(sym.at[dest(d, k), :, pl.ds(0, RA)], ra_buf.at[d, k], (ra_s, ra_r), (d, k), zdev[d])

    def ra_step(k):
        for d in range(2):
            if k > 0:
                ra_copy(d, k - 1).wait_recv()
                t = dest(d, k)
                if k == 1:
                    sym[t, d, :RA, :] = sym[t, d, :RA, :] + ra_buf[d, 0, d]
                else:
                    sym[t, :, :RA, :] = sym[t, :, :RA, :] + ra_buf[d, k - 1]
            if k < 4:
                ra_copy(d, k).start()

    def ra_swap():
        return rc(sym.at[z, 1 - x, pl.ds(0, RA)], rx_buf, (rx_s, rx_r), (0,), xdev)

    def bx_copy(m):
        return rc(sym.at[(z + m) % NZ, 1 - x, pl.ds(RA, RB)], bx_buf.at[m], (bx_s, bx_r), (m,), xdev)

    def bx_add(m):
        bx_copy(m).wait_recv()
        t = (z + m) % NZ
        sym[t, x, RA:, :] = sym[t, x, RA:, :] + bx_buf[m]

    def rb_copy(d, k):
        if k == 0:
            part = pl.ds(d * (RB // 2), RB // 2)
            return rc(sym.at[dest(d, k), x, pl.ds(RA + d * (RB // 2), RB // 2)], rb_buf.at[d, k, part], (rb_s, rb_r), (d, k), zdev[d])
        return rc(sym.at[dest(d, k), x, pl.ds(RA, RB)], rb_buf.at[d, k], (rb_s, rb_r), (d, k), zdev[d])

    def rb_step(k):
        if k == 0:
            bx_add(4)
        elif k < 4:
            bx_add(4 - k)
            bx_add(4 + k)
        else:
            bx_add(0)
        for d in range(2):
            if k > 0:
                rb_copy(d, k - 1).wait_recv()
                t = dest(d, k)
                if k == 1:
                    lo = d * (RB // 2)
                    hi = lo + RB // 2
                    sym[t, x, RA + lo:RA + hi, :] = sym[t, x, RA + lo:RA + hi, :] + rb_buf[d, 0, lo:hi, :]
                else:
                    sym[t, x, RA:, :] = sym[t, x, RA:, :] + rb_buf[d, k - 1]
            if k < 4:
                rb_copy(d, k).start()

    def count(f, carry):
        rows = [pl_buf[pl.ds(l * F + f, 1), :].astype(BF16) for l in range(L)]
        for ch in range(4):
            io = iota_buf[ch * 128:(ch + 1) * 128, :]
            hits = [jnp.where(io == rows[l], jnp.ones((), BF16), jnp.zeros((), BF16)) for l in range(L)]
            acc = (hits[0] + hits[1]) + (hits[2] + hits[3])
            cnt[f, ch * 128:(ch + 1) * 128, :] = acc
        return carry

    def counts(lo, hi):
        lax.fori_loop(lo, hi, count, 0)

    def w_copy(cb):
        return rc(wt.at[cb, 1 - core], wx.at[cb], (wx_s, wx_r), (cb,), cdev)

    def w_mul(m):
        g_inter.arrived(m)
        zz = (z + m) % NZ
        r = jnp.dot(ig[zz].reshape(2 * IR, SB), og[...], preferred_element_type=F32)
        for q in range(2):
            cb = zz * 2 + q
            for cc in range(2):
                wt[cb, cc] = r[q * IR + cc * WR:q * IR + (cc + 1) * WR]
            w_copy(cb).start()

    def wy_copy(o, h, dev):
        return pltpu.make_async_remote_copy(
            src_ref=ws.at[(y + o) % NY, h], dst_ref=wr.at[o, h], send_sem=wy_s.at[o, h], recv_sem=wy_r.at[o, h],
            device_id=dev, device_id_type=MESH,
        )

    def w_add(m):
        zz = (z + m) % NZ
        for q in range(2):
            cb = zz * 2 + q
            w_copy(cb).wait_recv()
            v = wt[cb, core] + wx[cb]
            h, yy = cb // NY, cb % NY
            ws[yy, h] = jnp.concatenate([v[:, :128], v[:, 128:]], axis=0).astype(BF16)
            o = (yy + NY - y) % NY

            @pl.when(o > 0)
            def _():
                wy_copy(o, h, smp_dev(xh, yy, core)).start()

    ra_step(0)
    for m in (4, 3, 5):
        bx_copy(m).start()
    g_inter.across(0, x).start()
    for n in (3, 4, 5):
        loads[n].wait()
    find_places()
    counts(0, 6)
    for j in range(F):
        v = pooled[j].astype(F32)
        pf[j] = v
        pf[j + F] = v
    g_inter.start_pair()
    counts(6, 10)
    ra_step(1)
    rb_step(0)
    bx_copy(2).start()
    bx_copy(6).start()
    g_inter.hop_first(1)
    g_inter.hop_second(1)
    w_mul(0)
    counts(10, 17)
    ra_step(2)
    rb_step(1)
    bx_copy(1).start()
    bx_copy(7).start()
    g_inter.hop_first(2)
    g_inter.hop_second(2)
    w_add(0)
    w_mul(1)
    w_mul(7)
    counts(17, 23)
    ra_step(3)
    rb_step(2)
    bx_copy(0).start()
    g_inter.hop_first(3)
    g_inter.hop_second(3)
    w_add(1)
    w_add(7)
    w_mul(2)
    w_mul(6)
    counts(23, 28)
    ra_step(4)
    ra_swap().start()
    rb_step(3)
    g_inter.hop_first(4)
    g_inter.hop_second(4)
    w_add(2)
    w_add(6)
    w_mul(3)
    w_mul(5)
    counts(28, 34)
    rb_step(4)
    ra_swap().wait_recv()
    gg[z, x, :RA, :] = (sym[z, x, :RA, :] + rx_buf[...]).astype(BF16)
    gg[z, x, RA:, :] = sym[z, x, RA:, :].astype(BF16)
    g_gram.start()
    g_gram.across(0, x).start()
    w_mul(4)
    w_add(3)
    w_add(5)
    g_gram.start_pair()
    counts(34, 41)
    w_add(4)
    g_gram.hop_first(1)
    g_gram.hop_first(2)
    counts(41, F)
    g_gram.hop_second(1)
    g_gram.hop_second(2)
    g_gram.hop_first(3)
    g_gram.hop_first(4)
    g_gram.hop_second(3)
    g_gram.hop_second(4)
    for m in range(NZ):
        g_gram.arrived(m)

    for at in range(0, OFF * F, 16):
        c, r0 = at // CH, at % CH
        v = gg[c // NX, c % NX, r0:r0 + 16, :].astype(F32)
        d, i0 = at // F, at % F
        for base in (d * 2 * F + i0, d * 2 * F + F + i0):
            cf[base:base + 16, :] = v

    row = lax.broadcasted_iota(I32, (8, 128), 0)
    lane = lax.broadcasted_iota(I32, (8, 128), 1)
    grp, low4 = lane >> 4, lane & 15
    turn_a = (((grp + row) & 7) << 4) | low4
    turn_b = (row - grp) & 7
    turn_c = (((row - grp) & 7) << 4) | low4

    def pooled_grad(i):
        accs = [jnp.zeros((E8, SB), F32) for _ in range(4)]
        n = 0
        for d in range(OFF):
            accs[n % 4] = accs[n % 4] + cf[pl.ds(i + d * 2 * F, 1), :] * pf[i + d]
            n += 1
        for d in range(1, OFF - 1):
            accs[n % 4] = accs[n % 4] + cf[pl.ds(i + (d * 2 * F + F - d), 1), :] * pf[i + (F - d)]
            n += 1
        v = (accs[0] + accs[1]) + (accs[2] + accs[3])
        hi = v.astype(BF16)
        lo = (v - hi.astype(F32)).astype(BF16)
        return jnp.concatenate([hi, lo], axis=0)

    def table_rows(f, fl, g, halves):
        r = lax.dot_general(halves, cnt[f], NT, preferred_element_type=F32)
        r = r[:E8] + r[E8:]
        for k in range(4):
            v = take(take(take(r[:, k * 128:(k + 1) * 128], turn_a, 1), turn_b, 0), turn_c, 1)
            td[g, k // 2, pl.ds((k % 2) * 128 + fl, 8, stride=GF), :] = v

    def tx_copy(g):
        return rc(td.at[g, 1 - core, pl.ds(0, 16 * GF)], tx.at[g], (tx_s, tx_r), (g,), cdev)

    def ty_copy(g, o, h):
        return rc(ts.at[g, (y + o) % NY, (xh + h) % 2], tr.at[g, o, h], (ty_s, ty_r), (g, o, h), ydev(o, h))

    def t_send(g):
        tx_copy(g).wait_recv()
        v = td[g, core, :16 * GF, :] + tx[g]
        ts[g] = v.astype(BF16).reshape(NY, 2, GF, 128)
        for o, h in others:
            ty_copy(g, o, h).start()

    def w_total():
        wtot = ws[y].astype(F32)
        for o in range(1, NY):
            for h in range(2):
                wy_copy(o, h, ydev(o)).wait_recv()
            wtot = wtot + wr[o].astype(F32)
        wf[...] = wtot
        ws[y] = wtot.astype(BF16)
        whc = rc(ws.at[y, 1 - xh], wxh, (wh_s, wh_r), (0,), hdev)
        whc.start()
        return whc

    halves = pooled_grad(0)
    for g in range(NG):
        def body(fl, halves, g=g):
            table_rows(g * GF + fl, fl, g, halves)
            return pooled_grad(g * GF + fl + 1)

        halves = lax.fori_loop(0, GF, body, halves, unroll=GF)
        tx_copy(g).start()
        if g > 0:
            t_send(g - 1)
    whc = w_total()
    t_send(NG - 1)

    for o in range(1, NY):
        for h in range(2):
            wy_copy(o, h, ydev(o)).wait_send()
    for copy in sent:
        copy.copy.wait_send()

    for g in range(NG):
        tot = ts[g, y, xh].astype(F32)
        for o, h in others:
            ty_copy(g, o, h).wait_recv()
            tot = tot + tr[g, o, h].astype(F32)
        t_out[g * GF:(g + 1) * GF, :] = tot
    whc.wait_recv()
    tot = wf[xh] + wxh[...].astype(F32)
    w_out[...] = tot


def finish(w_sum, t_sum, w_out, t_out):
    w_out[:, :128] = w_sum[:WR]
    w_out[:, 128:] = w_sum[WR:]
    t_out[...] = t_sum[...].T.reshape(E8, 16, F)


def shards(interaction, out_grad, top_weight, pooled, bags, row_place):
    dma = pltpu.SemaphoreType.DMA
    v = pltpu.VMEM
    vmem = pl.BlockSpec(memory_space=pltpu.VMEM)
    gather_sems = [dma(n) for n in ((2, 4), (NZ,), (2, 2, 4), (1,)) for _ in range(2)]
    outs = pl.pallas_call(
        kernel,
        out_shape=(
            jax.ShapeDtypeStruct((2 * WR, 128), F32),
            jax.ShapeDtypeStruct((F, 128), F32),
        ),
        in_specs=[pl.BlockSpec(memory_space=pl.ANY)] * 6,
        out_specs=(vmem, vmem),
        scratch_shapes=[
            v((SB, HB), BF16), v((F * F, HB), BF16), v((F, E8, SB), BF16), v((F, L, SB), I32), v((F, RT), I32),
            v((2, EXT * (EXT + 2), 128), F32),
            v((NZ, NX, CH, SB), F32),
            v((2, 4, NX, RA, SB), F32),
            v((2, 4, RB, SB), F32),
            v((NZ, RB, SB), F32),
            v((RA, SB), F32),
            v((NZ, NX, CH, SB), BF16),
            v((OFF * 2 * F, SB), F32),
            v((2 * F, E8, SB), F32),
            v((L * F, SB), F32),
            v((RT, SB), BF16),
            v((F, RT, SB), BF16),
            v((NZ, NX, IR, SB), BF16),
            v((16, 2, WR, HB), F32),
            v((16, WR, HB), F32),
            v((NY, 2, 2 * WR, 128), BF16),
            v((NY, 2, 2 * WR, 128), BF16),
            v((2, 2 * WR, 128), F32),
            v((2 * WR, 128), BF16),
            v((NG, 2, 17 * GF, 128), F32),
            v((NG, 16 * GF, 128), F32),
            v((NG, NY, 2, GF, 128), BF16),
            v((NG, NY, 2, GF, 128), BF16),
            dma((2, 4)), dma((2, 4)), dma((2, 4)), dma((2, 4)), dma((NZ,)), dma((NZ,)), dma((1,)), dma((1,)),
            *gather_sems, *gather_sems,
            dma((16,)), dma((16,)), dma((NY, 2)), dma((NY, 2)), dma((1,)), dma((1,)),
            dma((NG,)), dma((NG,)), dma((NG, NY, 2)), dma((NG, NY, 2)),
            dma((6,)),
        ],
        compiler_params=pltpu.CompilerParams(
            collective_id=0, has_side_effects=True, vmem_limit_bytes=56 * 1024 * 1024
        ),
    )(interaction, out_grad, top_weight, pooled, bags, row_place)
    weights, tables = pl.pallas_call(
        finish,
        out_shape=(
            jax.ShapeDtypeStruct((WR, HB), F32),
            jax.ShapeDtypeStruct((E8, 16, F), F32),
        ),
        in_specs=[vmem, vmem],
        out_specs=(vmem, vmem),
    )(*outs)
    return weights, jnp.transpose(tables, (0, 2, 1))


def solution(mesh):
    in_specs = (
        P("col", "sample"),
        P("sample", "col"),
        P(None, "col"),
        P(None, "col", "sample"),
        P(None, None, "sample"),
        P(),
    )
    out_specs = (P("sample", "col"), P("col", None, "sample"))
    return jax.shard_map(shards, mesh=mesh, in_specs=in_specs, out_specs=out_specs, check_vma=False)
```
